128 devices in a mesh: ep: 64 (over z, y, x), hd: 2 (over core).
Axes of the slice: x: 4, y: 4, z: 4, core: 2. Of those that a mesh axis runs over, the one named last changes fastest.
Arguments:
- hidden_in: bfloat16 [512, 3, 2048], P('ep'), may hold values from -6 to 6
- new_queries: bfloat16 [512, 3, 16, 128], P('ep', None, 'hd'), may hold values from -6 to 6
- new_keys: bfloat16 [512, 3, 16, 128], P('ep', None, 'hd'), may hold values from -6 to 6
- new_values: bfloat16 [512, 3, 32, 128], P('ep', None, 'hd'), may hold values from -6 to 6
- out_gate: bfloat16 [512, 3, 32, 128], P('ep', None, 'hd'), may hold values from -6 to 6
- decay_logit: bfloat16 [512, 3, 32], P('ep', None, 'hd'), may hold values from -6 to 6
- write_logit: bfloat16 [512, 3, 32], P('ep', None, 'hd'), may hold values from -6 to 6
- decay_scale: float32 [32], P('hd'), may hold values from -2 to 1.5
- decay_bias: float32 [32], P('hd'), may hold values from -2 to 1
- head_gain: float32 [128], replicated, may hold values from 0.1 to 1.9
- out_projection: bfloat16 [4096, 2048], P('hd'), may hold values from -0.09375 to 0.09375
- norm_gain: float32 [2048], replicated, may hold values from 0.1 to 1.9
- expert_ids: int32 [512, 3, 10], P('ep'), may hold values from 0 to 127, all different within a row; in each aligned block of 24 rows (0 to 23, 24 to 47, ..., all dimensions but the last counted through in order) at most 3 rows name the same one
- route_weight: float32 [512, 3, 10], P('ep'), may hold values from 0.02 to 1
- gate_weight: bfloat16 [128, 2048, 512], P(('ep', 'hd')), may hold values from -0.125 to 0.125
- up_weight: bfloat16 [128, 2048, 512], P(('ep', 'hd')), may hold values from -0.125 to 0.125
- down_weight: bfloat16 [128, 512, 2048], P(('ep', 'hd')), may hold values from -0.25 to 0.25
- old_state: float32 [512, 32, 128, 128], P('ep', 'hd'), may hold values from -4 to 4
Outputs:
- output_rows: bfloat16 [512, 3, 2048], P('ep', None, 'hd')
- new_state: float32 [512, 32, 128, 128], P('ep', 'hd')
The draws below stay inside these ranges and needn't reach their ends.
Inputs may be any that keep to these rules, and one draw needn't show every extreme that they name: `expert_ids`: each token names 10 different experts. Within each block of 24 tokens (the rows of one index of ep), no expert is named by more than 3 tokens, a bound that some block reaches.
All inputs are finite; a program needn't handle non-finite values.
Results may differ from the reference program's by a relative error of at most 0.013.
Values may be sent and summed in bfloat16 or wider, within the bound.
No kernel may reach another device: no remote copies, remote signals or barrier semaphores. Data moves between devices by JAX's collectives and lax.ppermute only.
A program may use at most 128 MiB of HBM per device.

```python
import math
import jax
import jax.numpy as jnp
import numpy as np
from jax import lax

D = 2048
HK = 16
HV = 32
DK = 128
DV = 128
FF = 512
TOPK = 10
STEPS = 3
ROWS_DEV = 8
ROWS = 512
GROUP_TOK = 24
EXPERTS = 128
CAP = 3
N_EP = 64


def block_scale(own_key, dims, cuts, low, largest):
    def one(dim, shards_of):
        heights = jax.random.uniform(jax.random.fold_in(jax.random.fold_in(own_key, 6), dim), (shards_of,), jnp.float32, low / len(cuts), largest / len(cuts))
        return jnp.repeat(jnp.exp(heights), dims[dim] // shards_of).reshape((-1,) + (1,) * (len(dims) - dim - 1))

    loudness = one(*cuts[0])
    for cut in cuts[1:]:
        loudness = loudness * one(*cut)
    return loudness


def routed_block(key, own, number, rows, count, top, most, lean):
    ranking = jax.random.permutation(key, count)
    crowded, usual = shares(count, rows * top, most, lean, True), shares(count, rows * top, most, lean, False)
    places = jnp.arange(count)

    def named(sizes, offset_by):
        used = int((sizes > 0).sum())
        fixed = max(1, used // 4)
        passed = fixed + (places - fixed + offset_by * (used - fixed)) % max(1, count - fixed)
        return jnp.zeros((count,), jnp.int32).at[ranking[jnp.where(places < fixed, places, passed)]].set(jnp.asarray(sizes, jnp.int32))

    sizes = jnp.where(number % 4 == 0, named(crowded, number // 4), named(usual, number - number // 4 - 1))
    mixed = jax.random.permutation(jax.random.fold_in(own, 3), count)
    giver, sink = mixed[0:count // 2 * 2:2], mixed[1:count // 2 * 2:2]
    room = jnp.minimum(sizes[giver] - 1, most - sizes[sink]) // 2
    room = jnp.where((giver == ranking[0]) | (sink == ranking[0]) | (sizes[sink] == 0), 0, jnp.maximum(room, 0))
    passed = jax.random.randint(jax.random.fold_in(own, 4), (count // 2,), 0, 1 << 20) % (room + 1)
    sizes = sizes.at[giver].add(-passed).at[sink].add(passed)
    labels = jnp.searchsorted(jnp.cumsum(sizes), jnp.arange(rows * top), side="right").astype(jnp.int32)
    listing = labels.reshape(top, rows).T
    listing = listing[jax.random.permutation(jax.random.fold_in(own, 1), rows)]
    offset_by = jax.random.randint(jax.random.fold_in(own, 2), (rows, 1), 0, top)
    return jnp.take_along_axis(listing, (jnp.arange(top)[None, :] + offset_by) % top, axis=1)


def shares(count, total, limit, slope, full):
    weights = [(1 << 20) // math.isqrt(standing ** slope) + 1 for standing in range(1, count + 1)]
    largest = limit if full else min(limit, max(-(-total // count), total * weights[0] // sum(weights)))
    least = 1 if total - largest >= count - 1 else 0
    given, surplus = [largest] + [least] * (count - 1), total - largest - least * (count - 1)
    while surplus > 0:
        free = [i for i in range(1, count) if given[i] < largest] or [i for i in range(1, count) if given[i] < limit]
        mass, left = sum([weights[i] for i in free]), surplus
        for i in free:
            extra = min(limit - given[i], max(1, left * weights[i] // mass), surplus)
            given[i] = given[i] + extra
            surplus = surplus - extra
    return np.array(given)


def bell_draw(key, extent, spread, bound, shards=(), kind=jnp.bfloat16):
    array = jax.random.normal(key, extent, jnp.float32) * spread
    if len(shards) > 0:
        array = block_scale(key, extent, shards, -0.22, 0.18) * array
    return jnp.clip(array, min=-bound, max=bound).astype(kind)


def setup_inputs(seed: int = 0) -> dict:
    seeds = jax.random.split(jax.random.key(seed), 19)
    hidden_in = bell_draw(seeds[0], (ROWS, STEPS, D), 1.0, 6.0, ((0, 64),))
    new_queries = bell_draw(seeds[1], (ROWS, STEPS, HK, DK), 1.0, 6.0, ((0, 64), (2, 2)))
    new_keys = bell_draw(seeds[2], (ROWS, STEPS, HK, DK), 1.0, 6.0, ((0, 64), (2, 2)))
    new_values = bell_draw(seeds[3], (ROWS, STEPS, HV, DV), 1.0, 6.0, ((0, 64), (2, 2)))
    out_gate = bell_draw(seeds[4], (ROWS, STEPS, HV, DV), 1.0, 6.0, ((0, 64), (2, 2)))
    decay_logit = bell_draw(seeds[5], (ROWS, STEPS, HV), 1.0, 6.0, ((0, 64), (2, 2)))
    write_logit = bell_draw(seeds[6], (ROWS, STEPS, HV), 1.0, 6.0, ((0, 64), (2, 2)))
    decay_scale = jnp.clip(-2.0 + 3.5 * jax.random.uniform(seeds[7], (HV,), jnp.float32) ** block_scale(seeds[7], (HV,), ((0, 2),), -0.2, 0.2), -2.0, 1.5)
    decay_bias = jnp.clip(-2.0 + 3.0 * jax.random.uniform(seeds[8], (HV,), jnp.float32) ** block_scale(seeds[8], (HV,), ((0, 2),), -0.2, 0.2), -2.0, 1.0)
    head_gain = jnp.clip(1.0 + 0.18 * jax.random.normal(seeds[9], (DV,), jnp.float32), 0.1, 1.9)
    out_projection = bell_draw(seeds[10], (HV * DV, D), (HV * DV) ** -0.5, 0.09375, ((0, 2),))
    norm_gain = jnp.clip(1.0 + 0.18 * jax.random.normal(seeds[11], (D,), jnp.float32), 0.1, 1.9)
    expert_ids_keys = jax.random.split(jax.random.fold_in(seeds[12], 1), ROWS * STEPS // GROUP_TOK)
    expert_ids_turns = jax.random.permutation(jax.random.fold_in(seeds[12], 3), ROWS * STEPS // GROUP_TOK)
    expert_ids = jax.vmap(lambda own, number: routed_block(jax.random.fold_in(seeds[12], 2), own, number, GROUP_TOK, EXPERTS, TOPK, CAP, 2))(expert_ids_keys, expert_ids_turns).reshape((ROWS, STEPS, TOPK))
    route_weight = jnp.clip(jnp.exp(math.log(1.0) - 3.912023 * jax.random.uniform(seeds[13], (ROWS, STEPS, TOPK), jnp.float32) ** block_scale(seeds[13], (ROWS, STEPS, TOPK), ((0, 64),), -0.2, 0.2)), 0.02, 1.0)
    gate_weight = bell_draw(seeds[14], (EXPERTS, D, FF), D ** -0.5, 0.125, ((0, 128),))
    up_weight = bell_draw(seeds[15], (EXPERTS, D, FF), D ** -0.5, 0.125, ((0, 128),))
    down_weight = bell_draw(seeds[16], (EXPERTS, FF, D), FF ** -0.5, 0.25, ((0, 128),))
    old_state = bell_draw(seeds[17], (ROWS, HV, DK, DV), 0.5, 4.0, ((0, 64), (1, 2)), jnp.float32)
    return {"hidden_in": hidden_in, "new_queries": new_queries, "new_keys": new_keys, "new_values": new_values, "out_gate": out_gate, "decay_logit": decay_logit, "write_logit": write_logit, "decay_scale": decay_scale, "decay_bias": decay_bias, "head_gain": head_gain, "out_projection": out_projection, "norm_gain": norm_gain, "expert_ids": expert_ids, "route_weight": route_weight, "gate_weight": gate_weight, "up_weight": up_weight, "down_weight": down_weight, "old_state": old_state}


EPSILON = 1e-06

def unit_rows(values_in):
    scaled = values_in.astype(jnp.float32)
    return scaled * lax.rsqrt(lax.optimization_barrier(jnp.sum(scaled * scaled, axis=-1, keepdims=True)) + EPSILON)

def delta_recurrence(running, new_queries, new_keys, new_values, decay_logit, write_logit, decay_scale, decay_bias):
    repeat = new_values.shape[2] // new_keys.shape[2]
    unit_queries = jnp.repeat(unit_rows(new_queries), repeat, axis=2)
    unit_keys = jnp.repeat(unit_rows(new_keys), repeat, axis=2)
    vectors = new_values.astype(jnp.float32)
    factor = jnp.exp(-jnp.exp(decay_scale) * jax.nn.softplus(decay_logit.astype(jnp.float32) + decay_bias))
    strength = jax.nn.sigmoid(write_logit.astype(jnp.float32))
    outputs = []
    for moment in range(unit_queries.shape[1]):
        running = running * factor[:, moment, :, None, None]
        recall = jnp.einsum('rhk,rhkv->rhv', unit_keys[:, moment], running, precision=lax.Precision.HIGHEST)
        update = strength[:, moment, :, None] * (vectors[:, moment] - recall)
        running = running + unit_keys[:, moment, :, :, None] * update[:, :, None, :]
        outputs.append(jnp.einsum('rhk,rhkv->rhv', unit_queries[:, moment], running, precision=lax.Precision.HIGHEST))
    return (jnp.stack(outputs, axis=1), running)

def head_output(core, out_gate, head_gain):
    normed_core = core * lax.rsqrt(lax.optimization_barrier(jnp.mean(core * core, axis=-1, keepdims=True)) + EPSILON) * head_gain
    return (normed_core * jax.nn.silu(out_gate.astype(jnp.float32))).astype(jnp.bfloat16)

def expert_ffn(rows_in, gate_matrix, up_matrix, down_matrix):
    gate_part = jnp.dot(rows_in, gate_matrix, preferred_element_type=jnp.float32)
    up_part = jnp.dot(rows_in, up_matrix, preferred_element_type=jnp.float32)
    activated = (jax.nn.silu(gate_part) * up_part).astype(jnp.bfloat16)
    return jnp.dot(activated, down_matrix, preferred_element_type=jnp.float32)

def slot_ranks(chosen):
    assignments = chosen.shape[0]
    places = jnp.arange(assignments, dtype=jnp.int32)
    earlier = (chosen[:, None] == chosen[None, :]) & (places[:, None] > places[None, :])
    return lax.optimization_barrier(jnp.sum(earlier.astype(jnp.int32), axis=1)).astype(jnp.int32)

def reference(hidden_in, new_queries, new_keys, new_values, out_gate, decay_logit, write_logit, decay_scale, decay_bias, head_gain, out_projection, norm_gain, expert_ids, route_weight, gate_weight, up_weight, down_weight, old_state):

    def one_group(pieces):
        running, queries_part, keys_part, values_part, gate_part, decay_part, write_part = pieces
        core, running = delta_recurrence(running, queries_part, keys_part, values_part, decay_part, write_part, decay_scale, decay_bias)
        return (head_output(core, gate_part, head_gain), running)
    grouped = tuple((piece.reshape((N_EP, ROWS_DEV) + piece.shape[1:]) for piece in (old_state, new_queries, new_keys, new_values, out_gate, decay_logit, write_logit)))
    heads_out, new_state = lax.map(one_group, grouped)
    new_state = new_state.reshape(old_state.shape)
    token_total = ROWS * STEPS
    residual = hidden_in.reshape(token_total, D).astype(jnp.float32) + jnp.dot(heads_out.reshape(token_total, HV * DV), out_projection, preferred_element_type=jnp.float32)
    normed = (residual * lax.rsqrt(lax.optimization_barrier(jnp.mean(residual * residual, axis=1, keepdims=True)) + EPSILON) * norm_gain).astype(jnp.bfloat16)
    chosen = expert_ids.reshape(N_EP, GROUP_TOK * TOPK)
    slot_rank = jax.vmap(slot_ranks)(chosen)
    position = (jnp.arange(N_EP, dtype=jnp.int32)[:, None] * CAP + slot_rank).reshape(-1).astype(jnp.int32)
    token_of = (jnp.arange(token_total * TOPK, dtype=jnp.int32) // TOPK).astype(jnp.int32)
    flat_ids = chosen.reshape(-1)
    buffers = jnp.zeros((EXPERTS, N_EP * CAP, D), jnp.bfloat16).at[flat_ids, position].set(normed[token_of])

    def one_expert(pieces):
        return expert_ffn(pieces[0], pieces[1], pieces[2], pieces[3])
    produced = lax.map(one_expert, (buffers, gate_weight, up_weight, down_weight))
    picked = produced[flat_ids, position].reshape(token_total, TOPK, D)
    mixing = (route_weight / lax.optimization_barrier(jnp.sum(route_weight, axis=2, keepdims=True))).reshape(token_total, TOPK)
    mixture = lax.optimization_barrier(jnp.sum(picked * mixing[:, :, None], axis=1))
    output_rows = (residual + mixture).astype(jnp.bfloat16).reshape(ROWS, STEPS, D)
    return (output_rows, new_state)
```

```python
import jax
import jax.numpy as jnp
from jax import lax
from jax.experimental import pallas as pl
from jax.experimental.pallas import tpu as pltpu
from jax.sharding import PartitionSpec as P

EPSILON = 1e-06
F32 = jnp.float32
BF16 = jnp.bfloat16

R = 8
T = 3
TOK = R * T
HK = 8
D = 2048
FF = 512
SLOTS = 3
CHIPS = 64
PARTS = 8
PC = D // PARTS
TP = 32
MiB = 1 << 20


def dot(a, b, dims=((1,), (0,))):
    return lax.dot_general(a, b, (dims, ((), ())), preferred_element_type=F32)


def iota(shape, dim):
    return lax.broadcasted_iota(jnp.int32, shape, dim)


def core_kernel(
    q_ref, k_ref, v_ref, g_ref, a_ref, b_ref, scale_ref, bias_ref, gain_ref, h_ref, s_ref, w_ref,
    own_ref, send_ref, ku_ref, uu_ref, f3_ref,
    qs, ks, vs, gs, fs, bs, acc,
):
    hk = pl.program_id(0)

    @pl.when(hk == 0)
    def _():
        for t in range(T):
            for r in range(R):
                at = t * R + r
                qs[pl.ds(at, HK, stride=TOK), :] = q_ref[r, t].astype(F32)
                ks[pl.ds(at, HK, stride=TOK), :] = k_ref[r, t].astype(F32)
                v = v_ref[r, t].astype(F32)
                g = g_ref[r, t].astype(F32)
                g = g * (1.0 / (1.0 + jnp.exp(-g)))
                for half in range(2):
                    rows = pl.ds(half * HK * TOK + at, HK, stride=TOK)
                    vs[rows, :] = v[half * HK : (half + 1) * HK]
                    gs[rows, :] = g[half * HK : (half + 1) * HK]
        rate = -jnp.exp(scale_ref[...])
        a_all = a_ref[...].astype(F32)
        b_all = b_ref[...].astype(F32)
        for t in range(T):
            x = a_all[:, t, :] + bias_ref[...]
            soft = jnp.maximum(x, 0.0) + jnp.log1p(jnp.exp(-jnp.abs(x)))
            factor = jnp.exp(rate * soft)
            strength = 1.0 / (1.0 + jnp.exp(-b_all[:, t, :]))
            for h in range(2 * HK):
                rows = slice(h * TOK + t * R, h * TOK + (t + 1) * R)
                fs[rows, :] = jnp.broadcast_to(factor[:, h : h + 1], (R, 128))
                bs[rows, :] = jnp.broadcast_to(strength[:, h : h + 1], (R, 128))

    rows = pl.ds(pl.multiple_of(hk * TOK, 8), TOK)
    q = qs[rows, :]
    k = ks[rows, :]
    q = q * lax.rsqrt(jnp.sum(q * q, axis=-1, keepdims=True) + EPSILON)
    k = k * lax.rsqrt(jnp.sum(k * k, axis=-1, keepdims=True) + EPSILON)
    ku_ref[0] = k
    kq = jnp.concatenate([k, q], axis=0)
    row_of = iota((2 * TOK, 128), 0) % R
    lhs = jnp.concatenate([jnp.where(row_of == r, kq, 0.0) for r in range(R)], axis=1).astype(BF16)

    kt = [k[t * R : (t + 1) * R] for t in range(T)]
    qt = [q[t * R : (t + 1) * R] for t in range(T)]

    def pair(x, y):
        return jnp.sum(x * y, axis=-1, keepdims=True)

    kk21, kk31, kk32 = pair(kt[1], kt[0]), pair(kt[2], kt[0]), pair(kt[2], kt[1])
    qk = [[pair(qt[t], kt[s]) for s in range(t + 1)] for t in range(T)]
    heads = []
    gain = gain_ref[...]
    for j in range(2):
        state = s_ref[:, j].reshape(R * 128, 128).astype(BF16)
        both = dot(lhs, state)
        recall = [both[t * R : (t + 1) * R] for t in range(T)]
        seen = [both[TOK + t * R : TOK + (t + 1) * R] for t in range(T)]
        base = pl.multiple_of((2 * hk + j) * TOK, 8)
        f = [fs[pl.ds(base + t * R, R), :] for t in range(T)]
        b = [bs[pl.ds(base + t * R, R), :] for t in range(T)]
        v = [vs[pl.ds(base + t * R, R), :] for t in range(T)]
        f01 = f[0] * f[1]
        f12 = f[1] * f[2]
        f012 = f01 * f[2]
        u0 = b[0] * (v[0] - f[0] * recall[0])
        u1 = b[1] * (v[1] - f01 * recall[1] - f[1] * kk21 * u0)
        u2 = b[2] * (v[2] - f012 * recall[2] - f12 * kk31 * u0 - f[2] * kk32 * u1)
        c0 = f[0] * seen[0] + qk[0][0] * u0
        c1 = f01 * seen[1] + f[1] * qk[1][0] * u0 + qk[1][1] * u1
        c2 = f012 * seen[2] + f12 * qk[2][0] * u0 + f[2] * qk[2][1] * u1 + qk[2][2] * u2
        lanes = slice(j * 128, (j + 1) * 128)
        uu_ref[0, :, lanes] = jnp.concatenate([f12 * u0, f[2] * u1, u2], axis=0)
        f3_ref[0, :, lanes] = f012
        c = jnp.concatenate([c0, c1, c2], axis=0)
        normed = c * lax.rsqrt(jnp.mean(c * c, axis=-1, keepdims=True) + EPSILON) * gain
        heads.append((normed * gs[pl.ds(base, TOK), :]).astype(BF16))
    part = dot(jnp.concatenate(heads, axis=1), w_ref[...])

    @pl.when(hk == 0)
    def _():
        acc[...] = part

    @pl.when(hk > 0)
    def _():
        acc[...] += part

    @pl.when(hk == HK - 1)
    def _():
        total = acc[...]
        send_ref[...] = total.astype(BF16)
        hidden = h_ref[...].astype(F32)
        for t in range(T):
            own_ref[t * R : (t + 1) * R, :] = total[t * R : (t + 1) * R] + hidden[:, t, :]


def core_call(q, k, v, g, a, b, scale, bias, gain, hidden, state, w):
    def whole(x):
        zeros = (0,) * x.ndim
        return pl.BlockSpec(x.shape, lambda i: zeros)

    small = (q, k, v, g, a, b, scale, bias, gain, hidden)
    return pl.pallas_call(
        core_kernel,
        grid=(HK,),
        in_specs=[whole(x) for x in small]
        + [
            pl.BlockSpec((R, 2, 128, 128), lambda i: (0, i, 0, 0)),
            pl.BlockSpec((256, D), lambda i: (i, 0)),
        ],
        out_specs=[
            pl.BlockSpec((TOK, D), lambda i: (0, 0)),
            pl.BlockSpec((TOK, D), lambda i: (0, 0)),
            pl.BlockSpec((1, TOK, 128), lambda i: (i, 0, 0)),
            pl.BlockSpec((1, TOK, 256), lambda i: (i, 0, 0)),
            pl.BlockSpec((1, R, 256), lambda i: (i, 0, 0)),
        ],
        out_shape=[
            jax.ShapeDtypeStruct((TOK, D), F32),
            jax.ShapeDtypeStruct((TOK, D), BF16),
            jax.ShapeDtypeStruct((HK, TOK, 128), F32),
            jax.ShapeDtypeStruct((HK, TOK, 256), F32),
            jax.ShapeDtypeStruct((HK, R, 256), F32),
        ],
        scratch_shapes=[
            pltpu.VMEM((HK * TOK, 128), F32),
            pltpu.VMEM((HK * TOK, 128), F32),
            pltpu.VMEM((2 * HK * TOK, 128), F32),
            pltpu.VMEM((2 * HK * TOK, 128), F32),
            pltpu.VMEM((2 * HK * TOK, 128), F32),
            pltpu.VMEM((2 * HK * TOK, 128), F32),
            pltpu.VMEM((TOK, D), F32),
        ],
        compiler_params=pltpu.CompilerParams(vmem_limit_bytes=24 * MiB),
        cost_estimate=pl.CostEstimate(flops=10**9, bytes_accessed=17 * MiB, transcendentals=10**5),
        name="core",
    )(*small, state, w)


def state_kernel(s_ref, k_ref, u_ref, f_ref, o_ref):
    def split(x):
        high = x.astype(BF16).astype(F32)
        return high, x - high

    k_high, k_low = split(k_ref[0])
    u_high, u_low = split(u_ref[0])
    keys = jnp.concatenate([k_high, k_low, k_high], axis=0).T
    updates = jnp.concatenate([u_high, u_high, u_low], axis=0).astype(BF16)
    row_of = iota(keys.shape, 1) % R
    for r in range(R):
        own = jnp.where(row_of == r, keys, 0.0).astype(BF16)
        added = dot(own, updates)
        for j in range(2):
            lanes = slice(j * 128, (j + 1) * 128)
            o_ref[r, j] = s_ref[r, j] * f_ref[0, r : r + 1, lanes] + added[:, lanes]


def state_call(state, keys, updates, factor):
    return pl.pallas_call(
        state_kernel,
        grid=(HK,),
        in_specs=[
            pl.BlockSpec((R, 2, 128, 128), lambda i: (0, i, 0, 0)),
            pl.BlockSpec((1, TOK, 128), lambda i: (i, 0, 0)),
            pl.BlockSpec((1, TOK, 256), lambda i: (i, 0, 0)),
            pl.BlockSpec((1, R, 256), lambda i: (i, 0, 0)),
        ],
        out_specs=pl.BlockSpec((R, 2, 128, 128), lambda i: (0, i, 0, 0)),
        out_shape=jax.ShapeDtypeStruct(state.shape, F32),
        compiler_params=pltpu.CompilerParams(vmem_limit_bytes=16 * MiB),
        cost_estimate=pl.CostEstimate(flops=10**9, bytes_accessed=17 * MiB, transcendentals=0),
        name="state",
    )(state, keys, updates, factor)


def table_kernel(ids_ref, route_ref, pick_ref, mix_ref):
    parity = lax.axis_index("hd")
    ids3 = ids_ref[...]
    route3 = route_ref[...]
    ids = jnp.concatenate([ids3[:, t, :] for t in range(T)], axis=0)
    route = jnp.concatenate([route3[:, t, :] for t in range(T)], axis=0)
    mixing = route / jnp.sum(route, axis=1, keepdims=True)
    expert = iota((TOK, CHIPS), 1) * 2 + parity
    named = jnp.zeros((TOK, CHIPS), F32)
    weight = jnp.zeros((TOK, CHIPS), F32)
    for c in range(ids.shape[1]):
        hit = ids[:, c : c + 1] == expert
        named = jnp.where(hit, 1.0, named)
        weight = jnp.where(hit, mixing[:, c : c + 1], weight)
    earlier = (iota((TOK, TOK), 0) > iota((TOK, TOK), 1)).astype(F32)
    rank = dot(earlier.astype(BF16), named.astype(BF16))
    rows = CHIPS * PARTS
    pad = jnp.zeros((TP - TOK, CHIPS), F32)
    spread = (iota((rows, CHIPS), 0) // PARTS == iota((rows, CHIPS), 1)).astype(F32).astype(BF16)
    across = (iota((CHIPS, rows), 1) // PARTS == iota((CHIPS, rows), 0)).astype(F32).astype(BF16)
    tile = (iota((TP, PARTS * TP), 1) % TP == iota((TP, PARTS * TP), 0)).astype(F32).astype(BF16)
    keep = iota((rows, PARTS * TP), 0) % PARTS == iota((rows, PARTS * TP), 1) // TP
    for s in range(SLOTS):
        here = jnp.where((named > 0.5) & (jnp.abs(rank - s) < 0.5), 1.0, 0.0)
        chosen = jnp.concatenate([here, pad], axis=0)
        tiled = dot(chosen.astype(BF16), tile, ((0,), (0,)))
        full = dot(spread, tiled.astype(BF16))
        pick_ref[s] = jnp.where(keep, full, 0.0).astype(BF16)
        share = jnp.concatenate([weight * here, pad], axis=0)
        high = share.astype(BF16).astype(F32)
        parts = jnp.concatenate([high, share - high], axis=0).astype(BF16)
        mix_ref[s] = dot(parts, across).astype(BF16)


def table_call(ids, route):
    return pl.pallas_call(
        table_kernel,
        out_shape=[
            jax.ShapeDtypeStruct((SLOTS, CHIPS * PARTS, PARTS * TP), BF16),
            jax.ShapeDtypeStruct((SLOTS, 2 * TP, CHIPS * PARTS), BF16),
        ],
        compiler_params=pltpu.CompilerParams(vmem_limit_bytes=16 * MiB),
        cost_estimate=pl.CostEstimate(flops=10**8, bytes_accessed=10**6, transcendentals=0),
        name="tables",
    )(ids, route)


def dispatch_kernel(own_ref, got_ref, gain_ref, pick_ref, res_ref, out_ref):
    residual = own_ref[...] + got_ref[...].astype(F32)
    res_ref[...] = residual
    scale = lax.rsqrt(jnp.mean(residual * residual, axis=1, keepdims=True) + EPSILON)
    normed = residual * scale * gain_ref[...]
    pad = jnp.zeros((TP - TOK, PC), F32)
    pieces = []
    for p in range(PARTS):
        pieces += [normed[:, p * PC : (p + 1) * PC], pad]
    stacked = jnp.concatenate(pieces, axis=0).astype(BF16)
    for s in range(SLOTS):
        out_ref[:, s * PC : (s + 1) * PC] = dot(pick_ref[s], stacked).astype(BF16)


def dispatch_call(own, got, gain, pick):
    return pl.pallas_call(
        dispatch_kernel,
        out_shape=[
            jax.ShapeDtypeStruct((TOK, D), F32),
            jax.ShapeDtypeStruct((CHIPS * PARTS, SLOTS * PC), BF16),
        ],
        compiler_params=pltpu.CompilerParams(vmem_limit_bytes=16 * MiB),
        cost_estimate=pl.CostEstimate(flops=2 * 10**8, bytes_accessed=2 * 10**6, transcendentals=0),
        name="dispatch",
    )(own, got, gain, pick)


def expert_kernel(x_ref, gate_ref, up_ref, down_ref, y_ref, wide):
    chunks = SLOTS * PC // 128
    for c in range(chunks):
        wide[c] = x_ref[:, c * 128 : (c + 1) * 128].astype(F32)
    gate = jnp.zeros((SLOTS * CHIPS, FF), F32)
    up = jnp.zeros((SLOTS * CHIPS, FF), F32)
    for p in range(PARTS):
        rows = [wide[c, pl.ds(p, CHIPS, stride=PARTS), :] for c in range(chunks)]
        x = jnp.concatenate(
            [jnp.concatenate(rows[0::2], axis=0), jnp.concatenate(rows[1::2], axis=0)], axis=1
        ).astype(BF16)
        gate += dot(x, gate_ref[0, p * PC : (p + 1) * PC, :])
        up += dot(x, up_ref[0, p * PC : (p + 1) * PC, :])
    activated = (gate * (1.0 / (1.0 + jnp.exp(-gate))) * up).astype(BF16)
    for p in range(PARTS):
        y = dot(activated, down_ref[0, :, p * PC : (p + 1) * PC])
        for c in range(chunks):
            at, side = c // 2 * CHIPS, c % 2 * 128
            wide[c, pl.ds(p, CHIPS, stride=PARTS), :] = y[at : at + CHIPS, side : side + 128]
    for c in range(chunks):
        y_ref[:, c * 128 : (c + 1) * 128] = wide[c].astype(BF16)


def expert_call(x, gate, up, down):
    return pl.pallas_call(
        expert_kernel,
        out_shape=jax.ShapeDtypeStruct(x.shape, BF16),
        scratch_shapes=[pltpu.VMEM((x.shape[1] // 128, x.shape[0], 128), F32)],
        compiler_params=pltpu.CompilerParams(vmem_limit_bytes=24 * MiB),
        cost_estimate=pl.CostEstimate(flops=12 * 10**8, bytes_accessed=8 * 10**6, transcendentals=10**5),
        name="expert",
    )(x, gate, up, down)


def combine_kernel(y_ref, mix_ref, res_ref, keep_ref, send_ref):
    parity = lax.axis_index("hd")
    part_of = iota((2 * TP, CHIPS * PARTS), 1) % PARTS
    half = D // 2
    total = None
    for s in range(SLOTS):
        mix = mix_ref[s].astype(F32)
        rows = [jnp.where(part_of == p, mix, 0.0) for p in range(PARTS)]
        lhs = jnp.concatenate(rows, axis=0).astype(BF16)
        one = dot(lhs, y_ref[:, s * PC : (s + 1) * PC])
        total = one if total is None else total + one
    parts = []
    for p in range(PARTS):
        at = p * 2 * TP
        parts.append(total[at : at + TOK] + total[at + TP : at + TP + TOK])
    low = jnp.concatenate(parts[: PARTS // 2], axis=1)
    high = jnp.concatenate(parts[PARTS // 2 :], axis=1)
    first = parity == 0
    keep_ref[...] = jnp.where(first, res_ref[:, :half] + low, res_ref[:, half:] + high)
    send_ref[...] = jnp.where(first, high, low).astype(BF16)


def combine_call(y, mix, residual):
    return pl.pallas_call(
        combine_kernel,
        out_shape=[
            jax.ShapeDtypeStruct((TOK, D // 2), F32),
            jax.ShapeDtypeStruct((TOK, D // 2), BF16),
        ],
        compiler_params=pltpu.CompilerParams(vmem_limit_bytes=24 * MiB),
        cost_estimate=pl.CostEstimate(flops=4 * 10**8, bytes_accessed=10**6, transcendentals=0),
        name="combine",
    )(y, mix, residual)


def final_kernel(keep_ref, got_ref, out_ref):
    total = keep_ref[...] + got_ref[...].astype(F32)
    steps = [total[t * R : (t + 1) * R] for t in range(T)]
    out_ref[...] = jnp.stack(steps, axis=1).astype(BF16)


def final_call(keep, got):
    return pl.pallas_call(
        final_kernel,
        out_shape=jax.ShapeDtypeStruct((R, T, D // 2), BF16),
        name="final",
    )(keep, got)


def local(
    hidden_in,
    new_queries,
    new_keys,
    new_values,
    out_gate,
    decay_logit,
    write_logit,
    decay_scale,
    decay_bias,
    head_gain,
    out_projection,
    norm_gain,
    expert_ids,
    route_weight,
    gate_weight,
    up_weight,
    down_weight,
    old_state,
):
    pick, mix = table_call(expert_ids, route_weight)
    own, send, keys, updates, factor = core_call(
        new_queries,
        new_keys,
        new_values,
        out_gate,
        decay_logit,
        write_logit,
        decay_scale.reshape(1, -1),
        decay_bias.reshape(1, -1),
        head_gain.reshape(1, -1),
        hidden_in,
        old_state,
        out_projection,
    )
    swap = [(0, 1), (1, 0)]
    got = lax.ppermute(send, "hd", swap)
    residual, outbound = dispatch_call(own, got, norm_gain.reshape(1, -1), pick)
    shape = (CHIPS, PARTS, SLOTS * PC)
    arrived = lax.all_to_all(outbound.reshape(shape), "ep", 0, 0, tiled=True)
    new_state = state_call(old_state, keys, updates, factor)
    produced = expert_call(arrived.reshape(outbound.shape), gate_weight, up_weight, down_weight)
    returned = lax.all_to_all(produced.reshape(shape), "ep", 0, 0, tiled=True)
    keep, give = combine_call(returned.reshape(outbound.shape), mix, residual)
    output_rows = final_call(keep, lax.ppermute(give, "hd", swap))
    return (output_rows, new_state)


def solution(mesh):
    in_specs = (
        P("ep", None, None),
        P("ep", None, "hd", None),
        P("ep", None, "hd", None),
        P("ep", None, "hd", None),
        P("ep", None, "hd", None),
        P("ep", None, "hd"),
        P("ep", None, "hd"),
        P("hd"),
        P("hd"),
        P(),
        P("hd", None),
        P(),
        P("ep", None, None),
        P("ep", None, None),
        P(("ep", "hd"), None, None),
        P(("ep", "hd"), None, None),
        P(("ep", "hd"), None, None),
        P("ep", "hd", None, None),
    )
    out_specs = (P("ep", None, "hd"), P("ep", "hd", None, None))
    return jax.shard_map(local, mesh=mesh, in_specs=in_specs, out_specs=out_specs, check_vma=False)
```

```python
import jax
import jax.numpy as jnp
from jax import lax
from jax.experimental import pallas as pl
from jax.experimental.pallas import tpu as pltpu
from jax.sharding import PartitionSpec as P

EPSILON = 1e-06
F32 = jnp.float32
BF16 = jnp.bfloat16

R = 8
T = 3
TOK = R * T
HK = 8
D = 2048
FF = 512
SLOTS = 3
CHIPS = 64
PARTS = 8
PC = D // PARTS
TP = 32
MiB = 1 << 20
CORE_VMEM = 55
GROUP = 8
AHEAD = 6
FLUSH_FIRST = (0, 1)
FLUSH_NEXT = (2, 3, 4)
FLUSH_LAST = (5, 6, 7)


def dot(a, b, dims=((1,), (0,))):
    return lax.dot_general(a, b, (dims, ((), ())), preferred_element_type=F32)


def iota(shape, dim):
    return lax.broadcasted_iota(jnp.int32, shape, dim)


def core_kernel(
    q_hbm, k_hbm, v_hbm, g_hbm, a_hbm, b_hbm, scale_hbm, bias_hbm, gain_hbm, h_hbm, s_hbm, w_hbm,
    own_ref, send_ref, state_ref,
    q_in, k_in, v_in, g_in, a_in, b_in, scale_in, bias_in, gain_in, h_in, w_in,
    qs, ks, vs, gs, fs, bs, lhs, seen, acc, small_sem, s_sem, w_sem,
):
    small = [
        pltpu.make_async_copy(source, target, small_sem.at[i])
        for i, (source, target) in enumerate(
            (
                (q_hbm, q_in),
                (k_hbm, k_in),
                (a_hbm, a_in),
                (b_hbm, b_in),
                (scale_hbm, scale_in),
                (bias_hbm, bias_in),
                (gain_hbm, gain_in),
                (v_hbm, v_in),
                (g_hbm, g_in),
                (h_hbm, h_in),
            )
        )
    ]
    state_in = [
        pltpu.make_async_copy(
            s_hbm.at[:, pl.ds(2 * i, 2)], state_ref.at[:, pl.ds(2 * i, 2)], s_sem.at[i]
        )
        for i in range(HK)
    ]
    weight_in = [
        pltpu.make_async_copy(
            w_hbm.at[pl.ds(i * 256, 256)], w_in.at[pl.ds(i * 256, 256)], w_sem.at[i]
        )
        for i in range(HK)
    ]
    stream = state_in + weight_in
    for copy in small + stream[:AHEAD]:
        copy.start()
    for copy in small:
        copy.wait()

    def arrive(n):
        stream[n].wait()
        if n + AHEAD < len(stream):
            stream[n + AHEAD].start()

    for t in range(T):
        for r in range(R):
            rows = pl.ds(t * HK * R + r, HK, stride=R)
            qs[rows, :] = q_in[r, t].astype(F32)
            ks[rows, :] = k_in[r, t].astype(F32)
            v = v_in[r, t].astype(F32)
            g = g_in[r, t].astype(F32)
            for half in range(2):
                rows = pl.ds((2 * t + half) * HK * R + r, HK, stride=R)
                vs[rows, :] = v[half * HK : (half + 1) * HK]
                gs[rows, :] = g[half * HK : (half + 1) * HK]
    rate = -jnp.exp(scale_in[...])
    for t in range(T):
        x = a_in[t].astype(F32) + bias_in[...]
        soft = jnp.maximum(x, 0.0) + jnp.log1p(jnp.exp(-jnp.abs(x)))
        factor = jnp.exp(rate * soft)
        strength = 1.0 / (1.0 + jnp.exp(-b_in[t].astype(F32)))
        for h in range(2 * HK):
            rows = slice((t * 2 * HK + h) * R, (t * 2 * HK + h + 1) * R)
            fs[rows, :] = jnp.broadcast_to(factor[:, h : h + 1], (R, 128))
            bs[rows, :] = jnp.broadcast_to(strength[:, h : h + 1], (R, 128))
    q = qs[...]
    k = ks[...]
    q = q * lax.rsqrt(jnp.sum(q * q, axis=-1, keepdims=True) + EPSILON)
    k = k * lax.rsqrt(jnp.sum(k * k, axis=-1, keepdims=True) + EPSILON)
    each = HK * R
    qt = [q[t * each : (t + 1) * each] for t in range(T)]
    kt = [k[t * each : (t + 1) * each] for t in range(T)]
    row_of = iota((2 * TOK, 128), 0) % R
    for i in range(HK):
        at = slice(i * R, (i + 1) * R)
        kq = jnp.concatenate([x[at] for x in kt + qt], axis=0)
        for r in range(R):
            lhs[i, :, r * 128 : (r + 1) * 128] = jnp.where(row_of == r, kq, 0.0).astype(BF16)

    def pair(x, y):
        return jnp.sum(x * y, axis=-1, keepdims=True)

    kk21, kk31, kk32 = pair(kt[1], kt[0]), pair(kt[2], kt[0]), pair(kt[2], kt[1])
    qk = [[pair(qt[t], kt[s]) for s in range(t + 1)] for t in range(T)]

    def split(x):
        high = x.astype(BF16).astype(F32)
        return high, x - high

    gain = gain_in[...]
    lane_of = iota((128, 3 * TOK), 1) % R
    outs = []
    for first in range(0, HK, GROUP):
        group = range(first, first + GROUP)
        span = slice(first * R, (first + GROUP) * R)
        for i in group:
            arrive(i)
            state = jnp.concatenate(
                [state_ref[:, 2 * i + j].reshape(R * 128, 128).astype(BF16) for j in range(2)],
                axis=1,
            )
            both = dot(lhs[i], state)
            for part in range(2 * T):
                seen[part, i * R : (i + 1) * R, :] = both[part * R : (part + 1) * R]

        k21, k31, k32 = kk21[span], kk31[span], kk32[span]
        qks = [[x[span] for x in row] for row in qk]
        late = []
        done = []
        for j in range(2):

            def of_heads(ref):
                return [
                    jnp.concatenate(
                        [ref[pl.ds((t * 2 * HK + 2 * i + j) * R, R), :] for i in group], axis=0
                    )
                    for t in range(T)
                ]

            lanes = slice(j * 128, (j + 1) * 128)
            f, b, v, gate = of_heads(fs), of_heads(bs), of_heads(vs), of_heads(gs)
            recall = [seen[t, span, lanes] for t in range(T)]
            look = [seen[T + t, span, lanes] for t in range(T)]
            f01 = f[0] * f[1]
            f12 = f[1] * f[2]
            f012 = f01 * f[2]
            u0 = b[0] * (v[0] - f[0] * recall[0])
            u1 = b[1] * (v[1] - f01 * recall[1] - f[1] * k21 * u0)
            u2 = b[2] * (v[2] - f012 * recall[2] - f12 * k31 * u0 - f[2] * k32 * u1)
            c0 = f[0] * look[0] + qks[0][0] * u0
            c1 = f01 * look[1] + f[1] * qks[1][0] * u0 + qks[1][1] * u1
            c2 = f012 * look[2] + f12 * qks[2][0] * u0 + f[2] * qks[2][1] * u1 + qks[2][2] * u2
            late.append((f12 * u0, f[2] * u1, u2, f012))
            ready = []
            for t, c in enumerate((c0, c1, c2)):
                normed = c * lax.rsqrt(jnp.mean(c * c, axis=-1, keepdims=True) + EPSILON) * gain
                ready.append(normed * (gate[t] * (1.0 / (1.0 + jnp.exp(-gate[t])))))
            done.append(ready)

        for i in group:
            at = slice((i - first) * R, (i - first + 1) * R)
            outs.append(
                jnp.concatenate(
                    [jnp.concatenate([x[at] for x in done[j]], axis=0) for j in range(2)], axis=1
                ).astype(BF16)
            )
            key_high, key_low = split(
                jnp.concatenate([x[i * R : (i + 1) * R] for x in kt], axis=0)
            )
            keys = jnp.concatenate([key_high, key_low, key_high], axis=0).T
            update = jnp.concatenate(
                [jnp.concatenate([x[at] for x in late[j][:3]], axis=0) for j in range(2)], axis=1
            )
            up_high, up_low = split(update)
            update = jnp.concatenate([up_high, up_high, up_low], axis=0).astype(BF16)
            for r in range(R):
                added = dot(jnp.where(lane_of == r, keys, 0.0).astype(BF16), update)
                row = (i - first) * R + r
                for j in range(2):
                    state_ref[r, 2 * i + j] = (
                        state_ref[r, 2 * i + j] * late[j][3][row : row + 1]
                        + added[:, j * 128 : (j + 1) * 128]
                    )
    for i in range(HK):
        arrive(HK + i)
        part = dot(outs[i], w_in[i * 256 : (i + 1) * 256, :])
        if i == 0:
            acc[...] = part
        elif i < HK - 1:
            acc[...] += part
        else:
            total = acc[...] + part
            send_ref[...] = total.astype(BF16)
            own_ref[...] = total + h_in[...].reshape(TOK, D).astype(F32)


def core_call(*args):
    args = [pltpu.with_memory_space_constraint(x, pltpu.HBM) for x in args]
    landing = [pltpu.VMEM(x.shape, x.dtype) for x in args[:10] + args[11:]]
    state = args[10]
    return pl.pallas_call(
        core_kernel,
        in_specs=[pl.BlockSpec(memory_space=pl.ANY)] * len(args),
        out_specs=[pl.BlockSpec(memory_space=pltpu.VMEM)] * 3,
        out_shape=[
            pltpu.VMEM((TOK, D), F32),
            pltpu.VMEM((TOK, D), BF16),
            pltpu.VMEM(state.shape, F32),
        ],
        scratch_shapes=landing
        + [pltpu.VMEM((HK * TOK, 128), F32)] * 2
        + [pltpu.VMEM((2 * HK * TOK, 128), F32)] * 4
        + [
            pltpu.VMEM((HK, 2 * TOK, R * 128), BF16),
            pltpu.VMEM((2 * T, HK * R, 256), F32),
            pltpu.VMEM((TOK, D), F32),
            pltpu.SemaphoreType.DMA((10,)),
            pltpu.SemaphoreType.DMA((HK,)),
            pltpu.SemaphoreType.DMA((HK,)),
        ],
        compiler_params=pltpu.CompilerParams(vmem_limit_bytes=CORE_VMEM * MiB),
        cost_estimate=pl.CostEstimate(flops=10**9, bytes_accessed=17 * MiB, transcendentals=10**5),
        name="core",
    )(*args)


def flush(state_ref, out_ref, sem, chunks):
    copies = []
    for n, i in enumerate(chunks):
        part = pl.ds(2 * i, 2)
        copies.append(pltpu.make_async_copy(state_ref.at[:, part], out_ref.at[:, part], sem.at[n]))
    for copy in copies:
        copy.start()
    return copies


def table_kernel(ids_ref, route_ref, state_ref, pick_ref, mix_ref, out_ref, sem):
    copies = flush(state_ref, out_ref, sem, FLUSH_FIRST)
    parity = lax.axis_index("hd")
    ids = ids_ref[...].reshape(TOK, -1)
    route = route_ref[...].reshape(TOK, -1)
    mixing = route / jnp.sum(route, axis=1, keepdims=True)
    expert = iota((TOK, CHIPS), 1) * 2 + parity
    named = jnp.zeros((TOK, CHIPS), F32)
    weight = jnp.zeros((TOK, CHIPS), F32)
    for c in range(ids.shape[1]):
        hit = ids[:, c : c + 1] == expert
        named = jnp.where(hit, 1.0, named)
        weight = jnp.where(hit, mixing[:, c : c + 1], weight)
    earlier = (iota((TOK, TOK), 0) > iota((TOK, TOK), 1)).astype(F32)
    rank = dot(earlier.astype(BF16), named.astype(BF16))
    rows = CHIPS * PARTS
    pad = jnp.zeros((TP - TOK, CHIPS), F32)
    spread = (iota((rows, CHIPS), 0) // PARTS == iota((rows, CHIPS), 1)).astype(F32).astype(BF16)
    across = (iota((CHIPS, rows), 1) // PARTS == iota((CHIPS, rows), 0)).astype(F32).astype(BF16)
    tile = (iota((TP, PARTS * TP), 1) % TP == iota((TP, PARTS * TP), 0)).astype(F32).astype(BF16)
    keep = iota((rows, PARTS * TP), 0) % PARTS == iota((rows, PARTS * TP), 1) // TP
    for s in range(SLOTS):
        here = jnp.where((named > 0.5) & (jnp.abs(rank - s) < 0.5), 1.0, 0.0)
        chosen = jnp.concatenate([here, pad], axis=0)
        tiled = dot(chosen.astype(BF16), tile, ((0,), (0,)))
        full = dot(spread, tiled.astype(BF16))
        pick_ref[s] = jnp.where(keep, full, 0.0).astype(BF16)
        share = jnp.concatenate([weight * here, pad], axis=0)
        high = share.astype(BF16).astype(F32)
        parts = jnp.concatenate([high, share - high], axis=0).astype(BF16)
        mix_ref[s] = dot(parts, across).astype(BF16)
    for copy in copies:
        copy.wait()


IN_VMEM = pl.BlockSpec(memory_space=pltpu.VMEM)
AS_IS = pl.BlockSpec(memory_space=pl.ANY)


def table_call(ids, route, state):
    return pl.pallas_call(
        table_kernel,
        in_specs=[IN_VMEM] * 2 + [AS_IS],
        out_specs=[IN_VMEM] * 2 + [AS_IS],
        out_shape=[
            jax.ShapeDtypeStruct((SLOTS, CHIPS * PARTS, PARTS * TP), BF16),
            jax.ShapeDtypeStruct((SLOTS, 2 * TP, CHIPS * PARTS), BF16),
            pltpu.HBM(state.shape, F32),
        ],
        scratch_shapes=[pltpu.SemaphoreType.DMA((len(FLUSH_FIRST),))],
        compiler_params=pltpu.CompilerParams(vmem_limit_bytes=16 * MiB),
        cost_estimate=pl.CostEstimate(flops=10**8, bytes_accessed=10**6, transcendentals=0),
        name="tables",
    )(ids, route, pltpu.with_memory_space_constraint(state, pltpu.VMEM))


def dispatch_kernel(own_ref, got_ref, gain_ref, pick_ref, res_ref, out_ref):
    residual = own_ref[...] + got_ref[...].astype(F32)
    res_ref[...] = residual
    scale = lax.rsqrt(jnp.mean(residual * residual, axis=1, keepdims=True) + EPSILON)
    normed = residual * scale * gain_ref[...]
    pad = jnp.zeros((TP - TOK, PC), F32)
    pieces = []
    for p in range(PARTS):
        pieces += [normed[:, p * PC : (p + 1) * PC], pad]
    stacked = jnp.concatenate(pieces, axis=0).astype(BF16)
    for s in range(SLOTS):
        out_ref[:, s * PC : (s + 1) * PC] = dot(pick_ref[s], stacked).astype(BF16)


def dispatch_call(own, got, gain, pick):
    return pl.pallas_call(
        dispatch_kernel,
        out_shape=[
            jax.ShapeDtypeStruct((TOK, D), F32),
            jax.ShapeDtypeStruct((CHIPS * PARTS, SLOTS * PC), BF16),
        ],
        compiler_params=pltpu.CompilerParams(vmem_limit_bytes=16 * MiB),
        cost_estimate=pl.CostEstimate(flops=2 * 10**8, bytes_accessed=2 * 10**6, transcendentals=0),
        name="dispatch",
    )(own, got, gain, pick)


def expert_kernel(
    x_ref, gate_ref, up_ref, down_ref, state_ref, held_ref, y_ref, out_ref, wide, sem
):
    copies = flush(state_ref, out_ref, sem, FLUSH_NEXT)
    chunks = SLOTS * PC // 128
    for c in range(chunks):
        wide[c] = x_ref[:, c * 128 : (c + 1) * 128].astype(F32)
    gate = jnp.zeros((SLOTS * CHIPS, FF), F32)
    up = jnp.zeros((SLOTS * CHIPS, FF), F32)
    for p in range(PARTS):
        rows = [wide[c, pl.ds(p, CHIPS, stride=PARTS), :] for c in range(chunks)]
        x = jnp.concatenate(
            [jnp.concatenate(rows[0::2], axis=0), jnp.concatenate(rows[1::2], axis=0)], axis=1
        ).astype(BF16)
        gate += dot(x, gate_ref[0, p * PC : (p + 1) * PC, :])
        up += dot(x, up_ref[0, p * PC : (p + 1) * PC, :])
    activated = (gate * (1.0 / (1.0 + jnp.exp(-gate))) * up).astype(BF16)
    for p in range(PARTS):
        y = dot(activated, down_ref[0, :, p * PC : (p + 1) * PC])
        for c in range(chunks):
            at, side = c // 2 * CHIPS, c % 2 * 128
            wide[c, pl.ds(p, CHIPS, stride=PARTS), :] = y[at : at + CHIPS, side : side + 128]
    for c in range(chunks):
        y_ref[:, c * 128 : (c + 1) * 128] = wide[c].astype(BF16)
    for copy in copies:
        copy.wait()


def expert_call(x, gate, up, down, state, held):
    return pl.pallas_call(
        expert_kernel,
        in_specs=[IN_VMEM] * 4 + [AS_IS] * 2,
        out_specs=[IN_VMEM, AS_IS],
        out_shape=[jax.ShapeDtypeStruct(x.shape, BF16), pltpu.HBM(state.shape, F32)],
        input_output_aliases={5: 1},
        scratch_shapes=[
            pltpu.VMEM((x.shape[1] // 128, x.shape[0], 128), F32),
            pltpu.SemaphoreType.DMA((len(FLUSH_NEXT),)),
        ],
        compiler_params=pltpu.CompilerParams(vmem_limit_bytes=24 * MiB),
        cost_estimate=pl.CostEstimate(
            flops=12 * 10**8, bytes_accessed=8 * 10**6, transcendentals=10**5
        ),
        name="expert",
    )(
        x,
        gate,
        up,
        down,
        pltpu.with_memory_space_constraint(state, pltpu.VMEM),
        pltpu.with_memory_space_constraint(held, pltpu.HBM),
    )


def combine_kernel(y_ref, mix_ref, res_ref, keep_ref, send_ref):
    parity = lax.axis_index("hd")
    part_of = iota((2 * TP, CHIPS * PARTS), 1) % PARTS
    half = D // 2
    total = None
    for s in range(SLOTS):
        mix = mix_ref[s].astype(F32)
        rows = [jnp.where(part_of == p, mix, 0.0) for p in range(PARTS)]
        lhs = jnp.concatenate(rows, axis=0).astype(BF16)
        one = dot(lhs, y_ref[:, s * PC : (s + 1) * PC])
        total = one if total is None else total + one
    parts = []
    for p in range(PARTS):
        at = p * 2 * TP
        parts.append(total[at : at + TOK] + total[at + TP : at + TP + TOK])
    low = jnp.concatenate(parts[: PARTS // 2], axis=1)
    high = jnp.concatenate(parts[PARTS // 2 :], axis=1)
    first = parity == 0
    keep_ref[...] = jnp.where(first, res_ref[:, :half] + low, res_ref[:, half:] + high)
    send_ref[...] = jnp.where(first, high, low).astype(BF16)


def combine_call(y, mix, residual):
    return pl.pallas_call(
        combine_kernel,
        out_shape=[
            jax.ShapeDtypeStruct((TOK, D // 2), F32),
            jax.ShapeDtypeStruct((TOK, D // 2), BF16),
        ],
        compiler_params=pltpu.CompilerParams(vmem_limit_bytes=24 * MiB),
        cost_estimate=pl.CostEstimate(flops=4 * 10**8, bytes_accessed=10**6, transcendentals=0),
        name="combine",
    )(y, mix, residual)


def last_kernel(state_ref, held_ref, out_ref, sem):
    for copy in flush(state_ref, out_ref, sem, FLUSH_LAST):
        copy.wait()


def last_call(state, held):
    return pl.pallas_call(
        last_kernel,
        in_specs=[AS_IS] * 2,
        out_specs=AS_IS,
        out_shape=pltpu.HBM(state.shape, F32),
        input_output_aliases={1: 0},
        scratch_shapes=[pltpu.SemaphoreType.DMA((len(FLUSH_LAST),))],
        compiler_params=pltpu.CompilerParams(vmem_limit_bytes=4 * MiB),
        cost_estimate=pl.CostEstimate(flops=0, bytes_accessed=6 * MiB, transcendentals=0),
        name="last",
    )(
        pltpu.with_memory_space_constraint(state, pltpu.VMEM),
        pltpu.with_memory_space_constraint(held, pltpu.HBM),
    )


def local(
    hidden_in,
    new_queries,
    new_keys,
    new_values,
    out_gate,
    decay_logit,
    write_logit,
    decay_scale,
    decay_bias,
    head_gain,
    out_projection,
    norm_gain,
    expert_ids,
    route_weight,
    gate_weight,
    up_weight,
    down_weight,
    old_state,
):
    def by_step(x):
        return jnp.transpose(x, (1, 0, 2))

    own, send, fresh = core_call(
        new_queries,
        new_keys,
        new_values,
        out_gate,
        by_step(decay_logit),
        by_step(write_logit),
        decay_scale.reshape(1, -1),
        decay_bias.reshape(1, -1),
        head_gain.reshape(1, -1),
        by_step(hidden_in),
        old_state,
        out_projection,
    )
    swap = [(0, 1), (1, 0)]
    got = lax.ppermute(send, "hd", swap)
    pick, mix, held = table_call(by_step(expert_ids), by_step(route_weight), fresh)
    residual, outbound = dispatch_call(own, got, norm_gain.reshape(1, -1), pick)
    shape = (CHIPS, PARTS, SLOTS * PC)
    arrived = lax.all_to_all(outbound.reshape(shape), "ep", 0, 0, tiled=True)
    produced, held = expert_call(
        arrived.reshape(outbound.shape), gate_weight, up_weight, down_weight, fresh, held
    )
    returned = lax.all_to_all(produced.reshape(shape), "ep", 0, 0, tiled=True)
    keep, give = combine_call(returned.reshape(outbound.shape), mix, residual)
    got = lax.ppermute(give, "hd", swap)
    new_state = last_call(fresh, held)
    total = keep + got.astype(F32)
    output_rows = by_step(total.astype(BF16).reshape(T, R, -1))
    return (output_rows, new_state)


def solution(mesh):
    in_specs = (
        P("ep", None, None),
        P("ep", None, "hd", None),
        P("ep", None, "hd", None),
        P("ep", None, "hd", None),
        P("ep", None, "hd", None),
        P("ep", None, "hd"),
        P("ep", None, "hd"),
        P("hd"),
        P("hd"),
        P(),
        P("hd", None),
        P(),
        P("ep", None, None),
        P("ep", None, None),
        P(("ep", "hd"), None, None),
        P(("ep", "hd"), None, None),
        P(("ep", "hd"), None, None),
        P("ep", "hd", None, None),
    )
    out_specs = (P("ep", None, "hd"), P("ep", "hd", None, None))
    return jax.shard_map(local, mesh=mesh, in_specs=in_specs, out_specs=out_specs, check_vma=False)
```

```python
import jax
import jax.numpy as jnp
from jax import lax
from jax.experimental import pallas as pl
from jax.experimental.pallas import tpu as pltpu
from jax.sharding import PartitionSpec as P

EPSILON = 1e-06
F32 = jnp.float32
BF16 = jnp.bfloat16

R = 8
T = 3
TOK = R * T
HK = 8
D = 2048
FF = 512
SLOTS = 3
CHIPS = 64
PARTS = 8
PC = D // PARTS
TP = 32
MiB = 1 << 20
CORE_VMEM = 55
GROUP = 2
AHEAD = 3
FLUSH_FIRST = (0, 1)
FLUSH_NEXT = (2, 3, 4)
FLUSH_LAST = (5, 6, 7)


def dot(a, b, dims=((1,), (0,))):
    return lax.dot_general(a, b, (dims, ((), ())), preferred_element_type=F32)


def iota(shape, dim):
    return lax.broadcasted_iota(jnp.int32, shape, dim)


def core_kernel(
    q_hbm, k_hbm, v_hbm, g_hbm, a_hbm, b_hbm, scale_hbm, bias_hbm, gain_hbm, h_hbm, s_hbm, w_hbm,
    own_ref, send_ref, state_ref,
    q_in, k_in, v_in, g_in, a_in, b_in, scale_in, bias_in, gain_in, h_in, w_in,
    qs, ks, vs, gs, fs, bs, lhs, seen, acc, small_sem, stream_sem,
):
    small = [
        pltpu.make_async_copy(source, target, small_sem.at[i])
        for i, (source, target) in enumerate(
            (
                (q_hbm, q_in),
                (k_hbm, k_in),
                (a_hbm, a_in),
                (b_hbm, b_in),
                (scale_hbm, scale_in),
                (bias_hbm, bias_in),
                (gain_hbm, gain_in),
                (v_hbm, v_in),
                (g_hbm, g_in),
                (h_hbm, h_in),
            )
        )
    ]
    stream = []
    for first in range(0, HK, GROUP):
        heads, rows = pl.ds(2 * first, 2 * GROUP), pl.ds(256 * first, 256 * GROUP)
        sems = (stream_sem.at[len(stream)], stream_sem.at[len(stream) + 1])
        stream += [
            pltpu.make_async_copy(s_hbm.at[:, heads], state_ref.at[:, heads], sems[0]),
            pltpu.make_async_copy(w_hbm.at[rows], w_in.at[rows], sems[1]),
        ]
    for copy in small + stream[:AHEAD]:
        copy.start()
    for copy in small:
        copy.wait()

    def arrive(n):
        stream[n].wait()
        if n + AHEAD < len(stream):
            stream[n + AHEAD].start()

    for t in range(T):
        for r in range(R):
            rows = pl.ds(t * HK * R + r, HK, stride=R)
            qs[rows, :] = q_in[r, t].astype(F32)
            ks[rows, :] = k_in[r, t].astype(F32)
            v = v_in[r, t].astype(F32)
            g = g_in[r, t].astype(F32)
            for half in range(2):
                rows = pl.ds((2 * t + half) * HK * R + r, HK, stride=R)
                vs[rows, :] = v[half * HK : (half + 1) * HK]
                gs[rows, :] = g[half * HK : (half + 1) * HK]
    rate = -jnp.exp(scale_in[...])
    for t in range(T):
        x = a_in[t].astype(F32) + bias_in[...]
        soft = jnp.maximum(x, 0.0) + jnp.log1p(jnp.exp(-jnp.abs(x)))
        factor = jnp.exp(rate * soft)
        strength = 1.0 / (1.0 + jnp.exp(-b_in[t].astype(F32)))
        for h in range(2 * HK):
            rows = slice((t * 2 * HK + h) * R, (t * 2 * HK + h + 1) * R)
            fs[rows, :] = jnp.broadcast_to(factor[:, h : h + 1], (R, 128))
            bs[rows, :] = jnp.broadcast_to(strength[:, h : h + 1], (R, 128))
    q = qs[...]
    k = ks[...]
    q = q * lax.rsqrt(jnp.sum(q * q, axis=-1, keepdims=True) + EPSILON)
    k = k * lax.rsqrt(jnp.sum(k * k, axis=-1, keepdims=True) + EPSILON)
    each = HK * R
    qt = [q[t * each : (t + 1) * each] for t in range(T)]
    kt = [k[t * each : (t + 1) * each] for t in range(T)]
    row_of = iota((2 * TOK, 128), 0) % R
    for i in range(HK):
        at = slice(i * R, (i + 1) * R)
        kq = jnp.concatenate([x[at] for x in kt + qt], axis=0)
        for r in range(R):
            lhs[i, :, r * 128 : (r + 1) * 128] = jnp.where(row_of == r, kq, 0.0).astype(BF16)

    def pair(x, y):
        return jnp.sum(x * y, axis=-1, keepdims=True)

    kk21, kk31, kk32 = pair(kt[1], kt[0]), pair(kt[2], kt[0]), pair(kt[2], kt[1])
    qk = [[pair(qt[t], kt[s]) for s in range(t + 1)] for t in range(T)]

    def split(x):
        high = x.astype(BF16).astype(F32)
        return high, x - high

    gain = gain_in[...]
    lane_of = iota((128, 3 * TOK), 1) % R
    outs = []
    for first in range(0, HK, GROUP):
        group = range(first, first + GROUP)
        span = slice(first * R, (first + GROUP) * R)
        arrive(2 * first // GROUP)
        for i in group:
            state = jnp.concatenate(
                [state_ref[:, 2 * i + j].reshape(R * 128, 128).astype(BF16) for j in range(2)],
                axis=1,
            )
            both = dot(lhs[i], state)
            for part in range(2 * T):
                seen[part, i * R : (i + 1) * R, :] = both[part * R : (part + 1) * R]

        k21, k31, k32 = kk21[span], kk31[span], kk32[span]
        qks = [[x[span] for x in row] for row in qk]
        late = []
        done = []
        for j in range(2):

            def of_heads(ref):
                return [
                    jnp.concatenate(
                        [ref[pl.ds((t * 2 * HK + 2 * i + j) * R, R), :] for i in group], axis=0
                    )
                    for t in range(T)
                ]

            lanes = slice(j * 128, (j + 1) * 128)
            f, b, v, gate = of_heads(fs), of_heads(bs), of_heads(vs), of_heads(gs)
            recall = [seen[t, span, lanes] for t in range(T)]
            look = [seen[T + t, span, lanes] for t in range(T)]
            f01 = f[0] * f[1]
            f12 = f[1] * f[2]
            f012 = f01 * f[2]
            u0 = b[0] * (v[0] - f[0] * recall[0])
            u1 = b[1] * (v[1] - f01 * recall[1] - f[1] * k21 * u0)
            u2 = b[2] * (v[2] - f012 * recall[2] - f12 * k31 * u0 - f[2] * k32 * u1)
            c0 = f[0] * look[0] + qks[0][0] * u0
            c1 = f01 * look[1] + f[1] * qks[1][0] * u0 + qks[1][1] * u1
            c2 = f012 * look[2] + f12 * qks[2][0] * u0 + f[2] * qks[2][1] * u1 + qks[2][2] * u2
            late.append((f12 * u0, f[2] * u1, u2, f012))
            ready = []
            for t, c in enumerate((c0, c1, c2)):
                normed = c * lax.rsqrt(jnp.mean(c * c, axis=-1, keepdims=True) + EPSILON) * gain
                ready.append(normed * (gate[t] * (1.0 / (1.0 + jnp.exp(-gate[t])))))
            done.append(ready)

        for i in group:
            at = slice((i - first) * R, (i - first + 1) * R)
            outs.append(
                jnp.concatenate(
                    [jnp.concatenate([x[at] for x in done[j]], axis=0) for j in range(2)], axis=1
                ).astype(BF16)
            )
            key_high, key_low = split(
                jnp.concatenate([x[i * R : (i + 1) * R] for x in kt], axis=0)
            )
            keys = jnp.concatenate([key_high, key_low, key_high], axis=0).T
            update = jnp.concatenate(
                [jnp.concatenate([x[at] for x in late[j][:3]], axis=0) for j in range(2)], axis=1
            )
            up_high, up_low = split(update)
            update = jnp.concatenate([up_high, up_high, up_low], axis=0).astype(BF16)
            for r in range(R):
                added = dot(jnp.where(lane_of == r, keys, 0.0).astype(BF16), update)
                row = (i - first) * R + r
                for j in range(2):
                    state_ref[r, 2 * i + j] = (
                        state_ref[r, 2 * i + j] * late[j][3][row : row + 1]
                        + added[:, j * 128 : (j + 1) * 128]
                    )
        arrive(2 * first // GROUP + 1)
        for i in group:
            part = dot(outs[i], w_in[i * 256 : (i + 1) * 256, :])
            if i == 0:
                acc[...] = part
            elif i < HK - 1:
                acc[...] += part
            else:
                total = acc[...] + part
                send_ref[...] = total.astype(BF16)
                own_ref[...] = total + h_in[...].reshape(TOK, D).astype(F32)


def core_call(*args):
    args = [pltpu.with_memory_space_constraint(x, pltpu.HBM) for x in args]
    landing = [pltpu.VMEM(x.shape, x.dtype) for x in args[:10] + args[11:]]
    state = args[10]
    return pl.pallas_call(
        core_kernel,
        in_specs=[pl.BlockSpec(memory_space=pl.ANY)] * len(args),
        out_specs=[pl.BlockSpec(memory_space=pltpu.VMEM)] * 3,
        out_shape=[
            pltpu.VMEM((TOK, D), F32),
            pltpu.VMEM((TOK, D), BF16),
            pltpu.VMEM(state.shape, F32),
        ],
        scratch_shapes=landing
        + [pltpu.VMEM((HK * TOK, 128), F32)] * 2
        + [pltpu.VMEM((2 * HK * TOK, 128), F32)] * 4
        + [
            pltpu.VMEM((HK, 2 * TOK, R * 128), BF16),
            pltpu.VMEM((2 * T, HK * R, 256), F32),
            pltpu.VMEM((TOK, D), F32),
            pltpu.SemaphoreType.DMA((10,)),
            pltpu.SemaphoreType.DMA((2 * HK // GROUP,)),
        ],
        compiler_params=pltpu.CompilerParams(vmem_limit_bytes=CORE_VMEM * MiB),
        cost_estimate=pl.CostEstimate(flops=10**9, bytes_accessed=17 * MiB, transcendentals=10**5),
        name="core",
    )(*args)


def flush(state_ref, out_ref, sem, chunks):
    copies = []
    for n, i in enumerate(chunks):
        part = pl.ds(2 * i, 2)
        copies.append(pltpu.make_async_copy(state_ref.at[:, part], out_ref.at[:, part], sem.at[n]))
    for copy in copies:
        copy.start()
    return copies


def table_kernel(ids_ref, route_ref, state_ref, pick_ref, mix_ref, out_ref, sem):
    copies = flush(state_ref, out_ref, sem, FLUSH_FIRST)
    parity = lax.axis_index("hd")
    ids = ids_ref[...].reshape(TOK, -1)
    route = route_ref[...].reshape(TOK, -1)
    mixing = route / jnp.sum(route, axis=1, keepdims=True)
    expert = iota((TOK, CHIPS), 1) * 2 + parity
    named = jnp.zeros((TOK, CHIPS), F32)
    weight = jnp.zeros((TOK, CHIPS), F32)
    for c in range(ids.shape[1]):
        hit = ids[:, c : c + 1] == expert
        named = jnp.where(hit, 1.0, named)
        weight = jnp.where(hit, mixing[:, c : c + 1], weight)
    earlier = (iota((TOK, TOK), 0) > iota((TOK, TOK), 1)).astype(F32)
    rank = dot(earlier.astype(BF16), named.astype(BF16))
    rows = CHIPS * PARTS
    pad = jnp.zeros((TP - TOK, CHIPS), F32)
    spread = (iota((rows, CHIPS), 0) // PARTS == iota((rows, CHIPS), 1)).astype(F32).astype(BF16)
    across = (iota((CHIPS, rows), 1) // PARTS == iota((CHIPS, rows), 0)).astype(F32).astype(BF16)
    tile = (iota((TP, PARTS * TP), 1) % TP == iota((TP, PARTS * TP), 0)).astype(F32).astype(BF16)
    keep = iota((rows, PARTS * TP), 0) % PARTS == iota((rows, PARTS * TP), 1) // TP
    for s in range(SLOTS):
        here = jnp.where((named > 0.5) & (jnp.abs(rank - s) < 0.5), 1.0, 0.0)
        chosen = jnp.concatenate([here, pad], axis=0)
        tiled = dot(chosen.astype(BF16), tile, ((0,), (0,)))
        full = dot(spread, tiled.astype(BF16))
        pick_ref[s] = jnp.where(keep, full, 0.0).astype(BF16)
        share = jnp.concatenate([weight * here, pad], axis=0)
        high = share.astype(BF16).astype(F32)
        parts = jnp.concatenate([high, share - high], axis=0).astype(BF16)
        mix_ref[s] = dot(parts, across).astype(BF16)
    for copy in copies:
        copy.wait()


IN_VMEM = pl.BlockSpec(memory_space=pltpu.VMEM)
AS_IS = pl.BlockSpec(memory_space=pl.ANY)


def table_call(ids, route, state):
    return pl.pallas_call(
        table_kernel,
        in_specs=[IN_VMEM] * 2 + [AS_IS],
        out_specs=[IN_VMEM] * 2 + [AS_IS],
        out_shape=[
            jax.ShapeDtypeStruct((SLOTS, CHIPS * PARTS, PARTS * TP), BF16),
            jax.ShapeDtypeStruct((SLOTS, 2 * TP, CHIPS * PARTS), BF16),
            pltpu.HBM(state.shape, F32),
        ],
        scratch_shapes=[pltpu.SemaphoreType.DMA((len(FLUSH_FIRST),))],
        compiler_params=pltpu.CompilerParams(vmem_limit_bytes=16 * MiB),
        cost_estimate=pl.CostEstimate(flops=10**8, bytes_accessed=10**6, transcendentals=0),
        name="tables",
    )(ids, route, pltpu.with_memory_space_constraint(state, pltpu.VMEM))


def dispatch_kernel(own_ref, got_ref, gain_ref, pick_ref, res_ref, out_ref):
    residual = own_ref[...] + got_ref[...].astype(F32)
    res_ref[...] = residual
    scale = lax.rsqrt(jnp.mean(residual * residual, axis=1, keepdims=True) + EPSILON)
    normed = residual * scale * gain_ref[...]
    pad = jnp.zeros((TP - TOK, PC), F32)
    pieces = []
    for p in range(PARTS):
        pieces += [normed[:, p * PC : (p + 1) * PC], pad]
    stacked = jnp.concatenate(pieces, axis=0).astype(BF16)
    for s in range(SLOTS):
        out_ref[:, s * PC : (s + 1) * PC] = dot(pick_ref[s], stacked).astype(BF16)


def dispatch_call(own, got, gain, pick):
    return pl.pallas_call(
        dispatch_kernel,
        out_shape=[
            jax.ShapeDtypeStruct((TOK, D), F32),
            jax.ShapeDtypeStruct((CHIPS * PARTS, SLOTS * PC), BF16),
        ],
        compiler_params=pltpu.CompilerParams(vmem_limit_bytes=16 * MiB),
        cost_estimate=pl.CostEstimate(flops=2 * 10**8, bytes_accessed=2 * 10**6, transcendentals=0),
        name="dispatch",
    )(own, got, gain, pick)


def expert_kernel(
    x_ref, gate_ref, up_ref, down_ref, state_ref, held_ref, y_ref, out_ref, wide, sem
):
    copies = flush(state_ref, out_ref, sem, FLUSH_NEXT)
    chunks = SLOTS * PC // 128
    for c in range(chunks):
        wide[c] = x_ref[:, c * 128 : (c + 1) * 128].astype(F32)
    gate = jnp.zeros((SLOTS * CHIPS, FF), F32)
    up = jnp.zeros((SLOTS * CHIPS, FF), F32)
    for p in range(PARTS):
        rows = [wide[c, pl.ds(p, CHIPS, stride=PARTS), :] for c in range(chunks)]
        x = jnp.concatenate(
            [jnp.concatenate(rows[0::2], axis=0), jnp.concatenate(rows[1::2], axis=0)], axis=1
        ).astype(BF16)
        gate += dot(x, gate_ref[0, p * PC : (p + 1) * PC, :])
        up += dot(x, up_ref[0, p * PC : (p + 1) * PC, :])
    activated = (gate * (1.0 / (1.0 + jnp.exp(-gate))) * up).astype(BF16)
    for p in range(PARTS):
        y = dot(activated, down_ref[0, :, p * PC : (p + 1) * PC])
        for c in range(chunks):
            at, side = c // 2 * CHIPS, c % 2 * 128
            wide[c, pl.ds(p, CHIPS, stride=PARTS), :] = y[at : at + CHIPS, side : side + 128]
    for c in range(chunks):
        y_ref[:, c * 128 : (c + 1) * 128] = wide[c].astype(BF16)
    for copy in copies:
        copy.wait()


def expert_call(x, gate, up, down, state, held):
    return pl.pallas_call(
        expert_kernel,
        in_specs=[IN_VMEM] * 4 + [AS_IS] * 2,
        out_specs=[IN_VMEM, AS_IS],
        out_shape=[jax.ShapeDtypeStruct(x.shape, BF16), pltpu.HBM(state.shape, F32)],
        input_output_aliases={5: 1},
        scratch_shapes=[
            pltpu.VMEM((x.shape[1] // 128, x.shape[0], 128), F32),
            pltpu.SemaphoreType.DMA((len(FLUSH_NEXT),)),
        ],
        compiler_params=pltpu.CompilerParams(vmem_limit_bytes=24 * MiB),
        cost_estimate=pl.CostEstimate(
            flops=12 * 10**8, bytes_accessed=8 * 10**6, transcendentals=10**5
        ),
        name="expert",
    )(
        x,
        gate,
        up,
        down,
        pltpu.with_memory_space_constraint(state, pltpu.VMEM),
        pltpu.with_memory_space_constraint(held, pltpu.HBM),
    )


def combine_kernel(y_ref, mix_ref, res_ref, keep_ref, send_ref):
    parity = lax.axis_index("hd")
    part_of = iota((2 * TP, CHIPS * PARTS), 1) % PARTS
    half = D // 2
    total = None
    for s in range(SLOTS):
        mix = mix_ref[s].astype(F32)
        rows = [jnp.where(part_of == p, mix, 0.0) for p in range(PARTS)]
        lhs = jnp.concatenate(rows, axis=0).astype(BF16)
        one = dot(lhs, y_ref[:, s * PC : (s + 1) * PC])
        total = one if total is None else total + one
    parts = []
    for p in range(PARTS):
        at = p * 2 * TP
        parts.append(total[at : at + TOK] + total[at + TP : at + TP + TOK])
    low = jnp.concatenate(parts[: PARTS // 2], axis=1)
    high = jnp.concatenate(parts[PARTS // 2 :], axis=1)
    first = parity == 0
    keep_ref[...] = jnp.where(first, res_ref[:, :half] + low, res_ref[:, half:] + high)
    send_ref[...] = jnp.where(first, high, low).astype(BF16)


def combine_call(y, mix, residual):
    return pl.pallas_call(
        combine_kernel,
        out_shape=[
            jax.ShapeDtypeStruct((TOK, D // 2), F32),
            jax.ShapeDtypeStruct((TOK, D // 2), BF16),
        ],
        compiler_params=pltpu.CompilerParams(vmem_limit_bytes=24 * MiB),
        cost_estimate=pl.CostEstimate(flops=4 * 10**8, bytes_accessed=10**6, transcendentals=0),
        name="combine",
    )(y, mix, residual)


def last_kernel(state_ref, held_ref, out_ref, sem):
    for copy in flush(state_ref, out_ref, sem, FLUSH_LAST):
        copy.wait()


def last_call(state, held):
    return pl.pallas_call(
        last_kernel,
        in_specs=[AS_IS] * 2,
        out_specs=AS_IS,
        out_shape=pltpu.HBM(state.shape, F32),
        input_output_aliases={1: 0},
        scratch_shapes=[pltpu.SemaphoreType.DMA((len(FLUSH_LAST),))],
        compiler_params=pltpu.CompilerParams(vmem_limit_bytes=4 * MiB),
        cost_estimate=pl.CostEstimate(flops=0, bytes_accessed=6 * MiB, transcendentals=0),
        name="last",
    )(
        pltpu.with_memory_space_constraint(state, pltpu.VMEM),
        pltpu.with_memory_space_constraint(held, pltpu.HBM),
    )


def local(
    hidden_in,
    new_queries,
    new_keys,
    new_values,
    out_gate,
    decay_logit,
    write_logit,
    decay_scale,
    decay_bias,
    head_gain,
    out_projection,
    norm_gain,
    expert_ids,
    route_weight,
    gate_weight,
    up_weight,
    down_weight,
    old_state,
):
    def by_step(x):
        return jnp.transpose(x, (1, 0, 2))

    own, send, fresh = core_call(
        new_queries,
        new_keys,
        new_values,
        out_gate,
        by_step(decay_logit),
        by_step(write_logit),
        decay_scale.reshape(1, -1),
        decay_bias.reshape(1, -1),
        head_gain.reshape(1, -1),
        by_step(hidden_in),
        old_state,
        out_projection,
    )
    swap = [(0, 1), (1, 0)]
    got = lax.ppermute(send, "hd", swap)
    pick, mix, held = table_call(by_step(expert_ids), by_step(route_weight), fresh)
    residual, outbound = dispatch_call(own, got, norm_gain.reshape(1, -1), pick)
    shape = (CHIPS, PARTS, SLOTS * PC)
    arrived = lax.all_to_all(outbound.reshape(shape), "ep", 0, 0, tiled=True)
    produced, held = expert_call(
        arrived.reshape(outbound.shape), gate_weight, up_weight, down_weight, fresh, held
    )
    returned = lax.all_to_all(produced.reshape(shape), "ep", 0, 0, tiled=True)
    keep, give = combine_call(returned.reshape(outbound.shape), mix, residual)
    got = lax.ppermute(give, "hd", swap)
    new_state = last_call(fresh, held)
    total = keep + got.astype(F32)
    output_rows = by_step(total.astype(BF16).reshape(T, R, -1))
    return (output_rows, new_state)


def solution(mesh):
    in_specs = (
        P("ep", None, None),
        P("ep", None, "hd", None),
        P("ep", None, "hd", None),
        P("ep", None, "hd", None),
        P("ep", None, "hd", None),
        P("ep", None, "hd"),
        P("ep", None, "hd"),
        P("hd"),
        P("hd"),
        P(),
        P("hd", None),
        P(),
        P("ep", None, None),
        P("ep", None, None),
        P(("ep", "hd"), None, None),
        P(("ep", "hd"), None, None),
        P(("ep", "hd"), None, None),
        P("ep", "hd", None, None),
    )
    out_specs = (P("ep", None, "hd"), P("ep", "hd", None, None))
    return jax.shard_map(local, mesh=mesh, in_specs=in_specs, out_specs=out_specs, check_vma=False)
```

```python
import jax
import jax.numpy as jnp
from jax import lax
from jax.experimental import pallas as pl
from jax.experimental.pallas import tpu as pltpu
from jax.sharding import PartitionSpec as P

EPSILON = 1e-06
F32 = jnp.float32
BF16 = jnp.bfloat16

R = 8
T = 3
TOK = R * T
HK = 8
D = 2048
FF = 512
SLOTS = 3
CHIPS = 64
PARTS = 8
PC = D // PARTS
TP = 32
MiB = 1 << 20
CORE_VMEM = 62
GROUP = 4
AHEAD = 2


def dot(a, b, dims=((1,), (0,))):
    return lax.dot_general(a, b, (dims, ((), ())), preferred_element_type=F32)


def iota(shape, dim):
    return lax.broadcasted_iota(jnp.int32, shape, dim)


def core_kernel(
    q_hbm, k_hbm, v_hbm, g_hbm, a_hbm, b_hbm, scale_hbm, bias_hbm, gain_hbm, h_hbm, s_hbm, w_hbm,
    own_ref, send_ref, k_hbm_out, u_hbm_out, f_hbm_out,
    q_in, k_in, v_in, g_in, a_in, b_in, scale_in, bias_in, gain_in, h_in, w_in, state_ref, ku_ref, uu_ref, f3_ref,
    qs, ks, vs, gs, fs, bs, lhs, seen, acc, small_sem, stream_sem, out_sem,
):
    small = [
        pltpu.make_async_copy(source, target, small_sem.at[i])
        for i, (source, target) in enumerate(
            (
                (q_hbm, q_in),
                (k_hbm, k_in),
                (a_hbm, a_in),
                (b_hbm, b_in),
                (scale_hbm, scale_in),
                (bias_hbm, bias_in),
                (gain_hbm, gain_in),
                (v_hbm, v_in),
                (g_hbm, g_in),
                (h_hbm, h_in),
            )
        )
    ]
    stream = []
    for first in range(0, HK, GROUP):
        heads, rows = pl.ds(2 * first, 2 * GROUP), pl.ds(256 * first, 256 * GROUP)
        sems = (stream_sem.at[len(stream)], stream_sem.at[len(stream) + 1])
        stream += [
            pltpu.make_async_copy(s_hbm.at[:, heads], state_ref.at[:, heads], sems[0]),
            pltpu.make_async_copy(w_hbm.at[rows], w_in.at[rows], sems[1]),
        ]
    for copy in small + stream[:AHEAD]:
        copy.start()
    for copy in small:
        copy.wait()

    def arrive(n):
        stream[n].wait()
        if n + AHEAD < len(stream):
            stream[n + AHEAD].start()

    for t in range(T):
        for r in range(R):
            rows = pl.ds(t * HK * R + r, HK, stride=R)
            qs[rows, :] = q_in[r, t].astype(F32)
            ks[rows, :] = k_in[r, t].astype(F32)
            v = v_in[r, t].astype(F32)
            g = g_in[r, t].astype(F32)
            for half in range(2):
                rows = pl.ds((2 * t + half) * HK * R + r, HK, stride=R)
                vs[rows, :] = v[half * HK : (half + 1) * HK]
                gs[rows, :] = g[half * HK : (half + 1) * HK]
    rate = -jnp.exp(scale_in[...])
    for t in range(T):
        x = a_in[t].astype(F32) + bias_in[...]
        soft = jnp.maximum(x, 0.0) + jnp.log1p(jnp.exp(-jnp.abs(x)))
        factor = jnp.exp(rate * soft)
        strength = 1.0 / (1.0 + jnp.exp(-b_in[t].astype(F32)))
        for h in range(2 * HK):
            rows = slice((t * 2 * HK + h) * R, (t * 2 * HK + h + 1) * R)
            fs[rows, :] = jnp.broadcast_to(factor[:, h : h + 1], (R, 128))
            bs[rows, :] = jnp.broadcast_to(strength[:, h : h + 1], (R, 128))
    q = qs[...]
    k = ks[...]
    q = q * lax.rsqrt(jnp.sum(q * q, axis=-1, keepdims=True) + EPSILON)
    k = k * lax.rsqrt(jnp.sum(k * k, axis=-1, keepdims=True) + EPSILON)
    each = HK * R
    qt = [q[t * each : (t + 1) * each] for t in range(T)]
    kt = [k[t * each : (t + 1) * each] for t in range(T)]
    row_of = iota((2 * TOK, 128), 0) % R
    for i in range(HK):
        at = slice(i * R, (i + 1) * R)
        kq = jnp.concatenate([x[at] for x in kt + qt], axis=0)
        for r in range(R):
            lhs[i, :, r * 128 : (r + 1) * 128] = jnp.where(row_of == r, kq, 0.0).astype(BF16)

    def pair(x, y):
        return jnp.sum(x * y, axis=-1, keepdims=True)

    kk21, kk31, kk32 = pair(kt[1], kt[0]), pair(kt[2], kt[0]), pair(kt[2], kt[1])
    qk = [[pair(qt[t], kt[s]) for s in range(t + 1)] for t in range(T)]

    gain = gain_in[...]
    outs = []
    written = []
    for first in range(0, HK, GROUP):
        group = range(first, first + GROUP)
        span = slice(first * R, (first + GROUP) * R)
        arrive(2 * first // GROUP)
        for i in group:
            state = jnp.concatenate(
                [state_ref[:, 2 * i + j].reshape(R * 128, 128).astype(BF16) for j in range(2)],
                axis=1,
            )
            both = dot(lhs[i], state)
            for part in range(2 * T):
                seen[part, i * R : (i + 1) * R, :] = both[part * R : (part + 1) * R]

        k21, k31, k32 = kk21[span], kk31[span], kk32[span]
        qks = [[x[span] for x in row] for row in qk]
        late = []
        done = []
        for j in range(2):

            def of_heads(ref):
                return [
                    jnp.concatenate(
                        [ref[pl.ds((t * 2 * HK + 2 * i + j) * R, R), :] for i in group], axis=0
                    )
                    for t in range(T)
                ]

            lanes = slice(j * 128, (j + 1) * 128)
            f, b, v, gate = of_heads(fs), of_heads(bs), of_heads(vs), of_heads(gs)
            recall = [seen[t, span, lanes] for t in range(T)]
            look = [seen[T + t, span, lanes] for t in range(T)]
            f01 = f[0] * f[1]
            f12 = f[1] * f[2]
            f012 = f01 * f[2]
            u0 = b[0] * (v[0] - f[0] * recall[0])
            u1 = b[1] * (v[1] - f01 * recall[1] - f[1] * k21 * u0)
            u2 = b[2] * (v[2] - f012 * recall[2] - f12 * k31 * u0 - f[2] * k32 * u1)
            c0 = f[0] * look[0] + qks[0][0] * u0
            c1 = f01 * look[1] + f[1] * qks[1][0] * u0 + qks[1][1] * u1
            c2 = f012 * look[2] + f12 * qks[2][0] * u0 + f[2] * qks[2][1] * u1 + qks[2][2] * u2
            late.append((f12 * u0, f[2] * u1, u2, f012))
            ready = []
            for t, c in enumerate((c0, c1, c2)):
                normed = c * lax.rsqrt(jnp.mean(c * c, axis=-1, keepdims=True) + EPSILON) * gain
                ready.append(normed * (gate[t] * (1.0 / (1.0 + jnp.exp(-gate[t])))))
            done.append(ready)

        for i in group:
            at = slice((i - first) * R, (i - first + 1) * R)
            outs.append(
                jnp.concatenate(
                    [jnp.concatenate([x[at] for x in done[j]], axis=0) for j in range(2)], axis=1
                ).astype(BF16)
            )
            ku_ref[i] = jnp.concatenate([x[i * R : (i + 1) * R] for x in kt], axis=0)
            for j in range(2):
                lanes = slice(j * 128, (j + 1) * 128)
                uu_ref[i, :, lanes] = jnp.concatenate([x[at] for x in late[j][:3]], axis=0)
                f3_ref[i, :, lanes] = late[j][3][at]
        for source, target in ((ku_ref, k_hbm_out), (uu_ref, u_hbm_out), (f3_ref, f_hbm_out)):
            span = pl.ds(first, GROUP)
            written.append(
                pltpu.make_async_copy(
                    source.at[span], target.at[span], out_sem.at[len(written)]
                )
            )
            written[-1].start()
        arrive(2 * first // GROUP + 1)
        for i in group:
            part = dot(outs[i], w_in[i * 256 : (i + 1) * 256, :])
            if i == 0:
                acc[...] = part
            elif i < HK - 1:
                acc[...] += part
            else:
                total = acc[...] + part
                send_ref[...] = total.astype(BF16)
                own_ref[...] = total + h_in[...].reshape(TOK, D).astype(F32)
    for copy in written:
        copy.wait()


def core_call(*args):
    args = [pltpu.with_memory_space_constraint(x, pltpu.HBM) for x in args]
    landing = [pltpu.VMEM(x.shape, x.dtype) for x in args[:10] + args[11:]]
    state = args[10]
    return pl.pallas_call(
        core_kernel,
        in_specs=[pl.BlockSpec(memory_space=pl.ANY)] * len(args),
        out_specs=[pl.BlockSpec(memory_space=pltpu.VMEM)] * 2
        + [pl.BlockSpec(memory_space=pl.ANY)] * 3,
        out_shape=[
            pltpu.VMEM((TOK, D), F32),
            pltpu.VMEM((TOK, D), BF16),
            pltpu.HBM((HK, TOK, 128), F32),
            pltpu.HBM((HK, TOK, 256), F32),
            pltpu.HBM((HK, R, 256), F32),
        ],
        scratch_shapes=landing
        + [pltpu.VMEM(state.shape, F32)]
        + [pltpu.VMEM((HK, rows, width), F32) for rows, width in ((TOK, 128), (TOK, 256), (R, 256))]
        + [pltpu.VMEM((HK * TOK, 128), F32)] * 2
        + [pltpu.VMEM((2 * HK * TOK, 128), F32)] * 4
        + [
            pltpu.VMEM((HK, 2 * TOK, R * 128), BF16),
            pltpu.VMEM((2 * T, HK * R, 256), F32),
            pltpu.VMEM((TOK, D), F32),
            pltpu.SemaphoreType.DMA((10,)),
            pltpu.SemaphoreType.DMA((2 * HK // GROUP,)),
            pltpu.SemaphoreType.DMA((3 * HK // GROUP,)),
        ],
        compiler_params=pltpu.CompilerParams(vmem_limit_bytes=CORE_VMEM * MiB),
        cost_estimate=pl.CostEstimate(flops=10**9, bytes_accessed=17 * MiB, transcendentals=10**5),
        name="core",
    )(*args)


def state_kernel(
    s_hbm, k_hbm, u_hbm, f_hbm, after_ref, o_hbm,
    state, k_in, u_in, f_in, small_sem, in_sem, out_sem,
):
    small = [
        pltpu.make_async_copy(source, target, small_sem.at[n])
        for n, (source, target) in enumerate(((k_hbm, k_in), (u_hbm, u_in), (f_hbm, f_in)))
    ]
    reads, writes = [], []
    for i in range(HK):
        heads = pl.ds(2 * i, 2)
        reads.append(pltpu.make_async_copy(s_hbm.at[:, heads], state.at[:, heads], in_sem.at[i]))
        writes.append(pltpu.make_async_copy(state.at[:, heads], o_hbm.at[:, heads], out_sem.at[i]))
    for copy in small + reads:
        copy.start()
    for copy in small:
        copy.wait()

    def split(x):
        high = x.astype(BF16).astype(F32)
        return high, x - high

    row_of = iota((128, 3 * TOK), 1) % R
    for i in range(HK):
        k_high, k_low = split(k_in[i])
        u_high, u_low = split(u_in[i])
        keys = jnp.concatenate([k_high, k_low, k_high], axis=0).T
        updates = jnp.concatenate([u_high, u_high, u_low], axis=0).astype(BF16)
        reads[i].wait()
        for r in range(R):
            own = jnp.where(row_of == r, keys, 0.0).astype(BF16)
            added = dot(own, updates)
            for j in range(2):
                lanes = slice(j * 128, (j + 1) * 128)
                state[r, 2 * i + j] = (
                    state[r, 2 * i + j] * f_in[i, r : r + 1, lanes] + added[:, lanes]
                )
        writes[i].start()
    for copy in writes:
        copy.wait()


def state_call(state, keys, updates, factor, after):
    args = [
        pltpu.with_memory_space_constraint(x, pltpu.HBM) for x in (state, keys, updates, factor)
    ]
    return pl.pallas_call(
        state_kernel,
        in_specs=[pl.BlockSpec(memory_space=pl.ANY)] * 5,
        out_specs=pl.BlockSpec(memory_space=pl.ANY),
        out_shape=pltpu.HBM(state.shape, F32),
        scratch_shapes=[pltpu.VMEM(x.shape, F32) for x in args]
        + [
            pltpu.SemaphoreType.DMA((3,)),
            pltpu.SemaphoreType.DMA((HK,)),
            pltpu.SemaphoreType.DMA((HK,)),
        ],
        compiler_params=pltpu.CompilerParams(vmem_limit_bytes=16 * MiB),
        cost_estimate=pl.CostEstimate(flops=10**9, bytes_accessed=17 * MiB, transcendentals=0),
        name="state",
    )(*args, pltpu.with_memory_space_constraint(after, pltpu.HBM))


def table_kernel(ids_ref, route_ref, state_ref, pick_ref, mix_ref):
    parity = lax.axis_index("hd")
    ids = ids_ref[...].reshape(TOK, -1)
    route = route_ref[...].reshape(TOK, -1)
    mixing = route / jnp.sum(route, axis=1, keepdims=True)
    expert = iota((TOK, CHIPS), 1) * 2 + parity
    named = jnp.zeros((TOK, CHIPS), F32)
    weight = jnp.zeros((TOK, CHIPS), F32)
    for c in range(ids.shape[1]):
        hit = ids[:, c : c + 1] == expert
        named = jnp.where(hit, 1.0, named)
        weight = jnp.where(hit, mixing[:, c : c + 1], weight)
    earlier = (iota((TOK, TOK), 0) > iota((TOK, TOK), 1)).astype(F32)
    rank = dot(earlier.astype(BF16), named.astype(BF16))
    rows = CHIPS * PARTS
    pad = jnp.zeros((TP - TOK, CHIPS), F32)
    spread = (iota((rows, CHIPS), 0) // PARTS == iota((rows, CHIPS), 1)).astype(F32).astype(BF16)
    across = (iota((CHIPS, rows), 1) // PARTS == iota((CHIPS, rows), 0)).astype(F32).astype(BF16)
    tile = (iota((TP, PARTS * TP), 1) % TP == iota((TP, PARTS * TP), 0)).astype(F32).astype(BF16)
    keep = iota((rows, PARTS * TP), 0) % PARTS == iota((rows, PARTS * TP), 1) // TP
    for s in range(SLOTS):
        here = jnp.where((named > 0.5) & (jnp.abs(rank - s) < 0.5), 1.0, 0.0)
        chosen = jnp.concatenate([here, pad], axis=0)
        tiled = dot(chosen.astype(BF16), tile, ((0,), (0,)))
        full = dot(spread, tiled.astype(BF16))
        pick_ref[s] = jnp.where(keep, full, 0.0).astype(BF16)
        share = jnp.concatenate([weight * here, pad], axis=0)
        high = share.astype(BF16).astype(F32)
        parts = jnp.concatenate([high, share - high], axis=0).astype(BF16)
        mix_ref[s] = dot(parts, across).astype(BF16)


def table_call(ids, route, state):
    return pl.pallas_call(
        table_kernel,
        in_specs=[pl.BlockSpec(memory_space=pltpu.VMEM)] * 2 + [pl.BlockSpec(memory_space=pl.ANY)],
        out_shape=[
            jax.ShapeDtypeStruct((SLOTS, CHIPS * PARTS, PARTS * TP), BF16),
            jax.ShapeDtypeStruct((SLOTS, 2 * TP, CHIPS * PARTS), BF16),
        ],
        compiler_params=pltpu.CompilerParams(vmem_limit_bytes=16 * MiB),
        cost_estimate=pl.CostEstimate(flops=10**8, bytes_accessed=10**6, transcendentals=0),
        name="tables",
    )(ids, route, pltpu.with_memory_space_constraint(state, pltpu.HBM))


def dispatch_kernel(own_ref, got_ref, gain_ref, pick_ref, res_ref, out_ref):
    residual = own_ref[...] + got_ref[...].astype(F32)
    res_ref[...] = residual
    scale = lax.rsqrt(jnp.mean(residual * residual, axis=1, keepdims=True) + EPSILON)
    normed = residual * scale * gain_ref[...]
    pad = jnp.zeros((TP - TOK, PC), F32)
    pieces = []
    for p in range(PARTS):
        pieces += [normed[:, p * PC : (p + 1) * PC], pad]
    stacked = jnp.concatenate(pieces, axis=0).astype(BF16)
    for s in range(SLOTS):
        out_ref[:, s * PC : (s + 1) * PC] = dot(pick_ref[s], stacked).astype(BF16)


def dispatch_call(own, got, gain, pick):
    return pl.pallas_call(
        dispatch_kernel,
        out_shape=[
            jax.ShapeDtypeStruct((TOK, D), F32),
            jax.ShapeDtypeStruct((CHIPS * PARTS, SLOTS * PC), BF16),
        ],
        compiler_params=pltpu.CompilerParams(vmem_limit_bytes=16 * MiB),
        cost_estimate=pl.CostEstimate(flops=2 * 10**8, bytes_accessed=2 * 10**6, transcendentals=0),
        name="dispatch",
    )(own, got, gain, pick)


def expert_kernel(x_ref, gate_ref, up_ref, down_ref, y_hbm, wide, y_out, sem):
    chunks = SLOTS * PC // 128
    for c in range(chunks):
        wide[c] = x_ref[:, c * 128 : (c + 1) * 128].astype(F32)
    gate = jnp.zeros((SLOTS * CHIPS, FF), F32)
    up = jnp.zeros((SLOTS * CHIPS, FF), F32)
    for p in range(PARTS):
        rows = [wide[c, pl.ds(p, CHIPS, stride=PARTS), :] for c in range(chunks)]
        x = jnp.concatenate(
            [jnp.concatenate(rows[0::2], axis=0), jnp.concatenate(rows[1::2], axis=0)], axis=1
        ).astype(BF16)
        gate += dot(x, gate_ref[0, p * PC : (p + 1) * PC, :])
        up += dot(x, up_ref[0, p * PC : (p + 1) * PC, :])
    activated = (gate * (1.0 / (1.0 + jnp.exp(-gate))) * up).astype(BF16)
    for p in range(PARTS):
        y = dot(activated, down_ref[0, :, p * PC : (p + 1) * PC])
        for c in range(chunks):
            at, side = c // 2 * CHIPS, c % 2 * 128
            wide[c, pl.ds(p, CHIPS, stride=PARTS), :] = y[at : at + CHIPS, side : side + 128]
    copies = []
    for c in range(chunks):
        lanes = slice(c * 128, (c + 1) * 128)
        y_out[:, lanes] = wide[c].astype(BF16)
        lanes = pl.ds(c * 128, 128)
        copies.append(pltpu.make_async_copy(y_out.at[:, lanes], y_hbm.at[:, lanes], sem.at[c]))
        copies[c].start()
    for copy in copies:
        copy.wait()


def expert_call(x, gate, up, down):
    return pl.pallas_call(
        expert_kernel,
        out_specs=pl.BlockSpec(memory_space=pl.ANY),
        out_shape=pltpu.HBM(x.shape, BF16),
        scratch_shapes=[
            pltpu.VMEM((x.shape[1] // 128, x.shape[0], 128), F32),
            pltpu.VMEM(x.shape, BF16),
            pltpu.SemaphoreType.DMA((x.shape[1] // 128,)),
        ],
        compiler_params=pltpu.CompilerParams(vmem_limit_bytes=24 * MiB),
        cost_estimate=pl.CostEstimate(
            flops=12 * 10**8, bytes_accessed=8 * 10**6, transcendentals=10**5
        ),
        name="expert",
    )(x, gate, up, down)


def combine_kernel(y_ref, mix_ref, res_ref, state_ref, keep_ref, send_ref, out_ref):
    parity = lax.axis_index("hd")
    part_of = iota((2 * TP, CHIPS * PARTS), 1) % PARTS
    half = D // 2
    total = None
    for s in range(SLOTS):
        mix = mix_ref[s].astype(F32)
        rows = [jnp.where(part_of == p, mix, 0.0) for p in range(PARTS)]
        lhs = jnp.concatenate(rows, axis=0).astype(BF16)
        one = dot(lhs, y_ref[:, s * PC : (s + 1) * PC])
        total = one if total is None else total + one
    parts = []
    for p in range(PARTS):
        at = p * 2 * TP
        parts.append(total[at : at + TOK] + total[at + TP : at + TP + TOK])
    low = jnp.concatenate(parts[: PARTS // 2], axis=1)
    high = jnp.concatenate(parts[PARTS // 2 :], axis=1)
    first = parity == 0
    keep_ref[...] = jnp.where(first, res_ref[:, :half] + low, res_ref[:, half:] + high)
    send_ref[...] = jnp.where(first, high, low).astype(BF16)


def combine_call(y, mix, residual, state):
    vmem = pl.BlockSpec(memory_space=pltpu.VMEM)
    held = pl.BlockSpec(memory_space=pl.ANY)
    return pl.pallas_call(
        combine_kernel,
        in_specs=[vmem, vmem, vmem, held],
        out_specs=[vmem, vmem, held],
        out_shape=[
            jax.ShapeDtypeStruct((TOK, D // 2), F32),
            jax.ShapeDtypeStruct((TOK, D // 2), BF16),
            pltpu.HBM(state.shape, F32),
        ],
        input_output_aliases={3: 2},
        compiler_params=pltpu.CompilerParams(vmem_limit_bytes=24 * MiB),
        cost_estimate=pl.CostEstimate(flops=4 * 10**8, bytes_accessed=10**6, transcendentals=0),
        name="combine",
    )(y, mix, residual, pltpu.with_memory_space_constraint(state, pltpu.HBM))


def local(
    hidden_in,
    new_queries,
    new_keys,
    new_values,
    out_gate,
    decay_logit,
    write_logit,
    decay_scale,
    decay_bias,
    head_gain,
    out_projection,
    norm_gain,
    expert_ids,
    route_weight,
    gate_weight,
    up_weight,
    down_weight,
    old_state,
):
    def by_step(x):
        return jnp.transpose(x, (1, 0, 2))

    own, send, keys, updates, factor = core_call(
        new_queries,
        new_keys,
        new_values,
        out_gate,
        by_step(decay_logit),
        by_step(write_logit),
        decay_scale.reshape(1, -1),
        decay_bias.reshape(1, -1),
        head_gain.reshape(1, -1),
        by_step(hidden_in),
        old_state,
        out_projection,
    )
    swap = [(0, 1), (1, 0)]
    got = lax.ppermute(send, "hd", swap)
    pick, mix = table_call(by_step(expert_ids), by_step(route_weight), old_state)
    residual, outbound = dispatch_call(own, got, norm_gain.reshape(1, -1), pick)
    shape = (CHIPS, PARTS, SLOTS * PC)
    arrived = lax.all_to_all(outbound.reshape(shape), "ep", 0, 0, tiled=True)
    produced = expert_call(arrived.reshape(outbound.shape), gate_weight, up_weight, down_weight)
    new_state = state_call(old_state, keys, updates, factor, produced)
    returned = lax.all_to_all(produced.reshape(shape), "ep", 0, 0, tiled=True)
    keep, give, new_state = combine_call(
        returned.reshape(outbound.shape), mix, residual, new_state
    )
    got = lax.ppermute(give, "hd", swap)
    total = keep + got.astype(F32)
    output_rows = by_step(total.astype(BF16).reshape(T, R, -1))
    return (output_rows, new_state)


def solution(mesh):
    in_specs = (
        P("ep", None, None),
        P("ep", None, "hd", None),
        P("ep", None, "hd", None),
        P("ep", None, "hd", None),
        P("ep", None, "hd", None),
        P("ep", None, "hd"),
        P("ep", None, "hd"),
        P("hd"),
        P("hd"),
        P(),
        P("hd", None),
        P(),
        P("ep", None, None),
        P("ep", None, None),
        P(("ep", "hd"), None, None),
        P(("ep", "hd"), None, None),
        P(("ep", "hd"), None, None),
        P("ep", "hd", None, None),
    )
    out_specs = (P("ep", None, "hd"), P("ep", "hd", None, None))
    return jax.shard_map(local, mesh=mesh, in_specs=in_specs, out_specs=out_specs, check_vma=False)
```

```python
import jax
import jax.numpy as jnp
from jax import lax
from jax.experimental import pallas as pl
from jax.experimental.pallas import tpu as pltpu
from jax.sharding import PartitionSpec as P

EPSILON = 1e-06
F32 = jnp.float32
BF16 = jnp.bfloat16

R = 8
T = 3
TOK = R * T
HK = 8
D = 2048
FF = 512
SLOTS = 3
CHIPS = 64
PARTS = 8
PC = D // PARTS
TP = 32
MiB = 1 << 20
CORE_VMEM = 62
GROUPS = (5, 3)
STARTS = tuple(sum(GROUPS[:n]) for n in range(len(GROUPS)))
AHEAD = 2


def dot(a, b, dims=((1,), (0,))):
    return lax.dot_general(a, b, (dims, ((), ())), preferred_element_type=F32)


def iota(shape, dim):
    return lax.broadcasted_iota(jnp.int32, shape, dim)


def core_kernel(
    q_hbm, k_hbm, v_hbm, g_hbm, a_hbm, b_hbm, scale_hbm, bias_hbm, gain_hbm, h_hbm, s_hbm, w_hbm,
    own_ref, send_ref, k_hbm_out, u_hbm_out, f_hbm_out,
    q_in, k_in, v_in, g_in, a_in, b_in, scale_in, bias_in, gain_in, h_in, w_in, state_ref, ku_ref, uu_ref, f3_ref,
    qs, ks, vs, gs, fs, bs, lhs, seen, acc, small_sem, stream_sem, out_sem,
):
    small = [
        pltpu.make_async_copy(source, target, small_sem.at[i])
        for i, (source, target) in enumerate(
            (
                (q_hbm, q_in),
                (k_hbm, k_in),
                (a_hbm, a_in),
                (b_hbm, b_in),
                (scale_hbm, scale_in),
                (bias_hbm, bias_in),
                (gain_hbm, gain_in),
                (v_hbm, v_in),
                (g_hbm, g_in),
                (h_hbm, h_in),
            )
        )
    ]
    stream = []
    for first, count in zip(STARTS, GROUPS):
        heads, rows = pl.ds(2 * first, 2 * count), pl.ds(256 * first, 256 * count)
        sems = (stream_sem.at[len(stream)], stream_sem.at[len(stream) + 1])
        stream += [
            pltpu.make_async_copy(s_hbm.at[:, heads], state_ref.at[:, heads], sems[0]),
            pltpu.make_async_copy(w_hbm.at[rows], w_in.at[rows], sems[1]),
        ]
    for copy in small + stream[:AHEAD]:
        copy.start()
    for copy in small:
        copy.wait()

    def arrive(n):
        stream[n].wait()
        if n + AHEAD < len(stream):
            stream[n + AHEAD].start()

    for t in range(T):
        for r in range(R):
            rows = pl.ds(t * HK * R + r, HK, stride=R)
            qs[rows, :] = q_in[r, t].astype(F32)
            ks[rows, :] = k_in[r, t].astype(F32)
            v = v_in[r, t].astype(F32)
            g = g_in[r, t].astype(F32)
            for half in range(2):
                rows = pl.ds((2 * t + half) * HK * R + r, HK, stride=R)
                vs[rows, :] = v[half * HK : (half + 1) * HK]
                gs[rows, :] = g[half * HK : (half + 1) * HK]
    rate = -jnp.exp(scale_in[...])
    for t in range(T):
        x = a_in[t].astype(F32) + bias_in[...]
        soft = jnp.maximum(x, 0.0) + jnp.log1p(jnp.exp(-jnp.abs(x)))
        factor = jnp.exp(rate * soft)
        strength = 1.0 / (1.0 + jnp.exp(-b_in[t].astype(F32)))
        for h in range(2 * HK):
            rows = slice((t * 2 * HK + h) * R, (t * 2 * HK + h + 1) * R)
            fs[rows, :] = jnp.broadcast_to(factor[:, h : h + 1], (R, 128))
            bs[rows, :] = jnp.broadcast_to(strength[:, h : h + 1], (R, 128))
    q = qs[...]
    k = ks[...]
    q = q * lax.rsqrt(jnp.sum(q * q, axis=-1, keepdims=True) + EPSILON)
    k = k * lax.rsqrt(jnp.sum(k * k, axis=-1, keepdims=True) + EPSILON)
    each = HK * R
    qt = [q[t * each : (t + 1) * each] for t in range(T)]
    kt = [k[t * each : (t + 1) * each] for t in range(T)]
    row_of = iota((2 * TOK, 128), 0) % R
    for i in range(HK):
        at = slice(i * R, (i + 1) * R)
        kq = jnp.concatenate([x[at] for x in kt + qt], axis=0)
        for r in range(R):
            lhs[i, :, r * 128 : (r + 1) * 128] = jnp.where(row_of == r, kq, 0.0).astype(BF16)

    def pair(x, y):
        return jnp.sum(x * y, axis=-1, keepdims=True)

    kk21, kk31, kk32 = pair(kt[1], kt[0]), pair(kt[2], kt[0]), pair(kt[2], kt[1])
    qk = [[pair(qt[t], kt[s]) for s in range(t + 1)] for t in range(T)]

    gain = gain_in[...]
    outs = []
    written = []
    for place, (first, count) in enumerate(zip(STARTS, GROUPS)):
        group = range(first, first + count)
        span = slice(first * R, (first + count) * R)
        arrive(2 * place)
        for i in group:
            state = jnp.concatenate(
                [state_ref[:, 2 * i + j].reshape(R * 128, 128).astype(BF16) for j in range(2)],
                axis=1,
            )
            both = dot(lhs[i], state)
            for part in range(2 * T):
                seen[part, i * R : (i + 1) * R, :] = both[part * R : (part + 1) * R]

        k21, k31, k32 = kk21[span], kk31[span], kk32[span]
        qks = [[x[span] for x in row] for row in qk]
        late = []
        done = []
        for j in range(2):

            def of_heads(ref):
                return [
                    jnp.concatenate(
                        [ref[pl.ds((t * 2 * HK + 2 * i + j) * R, R), :] for i in group], axis=0
                    )
                    for t in range(T)
                ]

            lanes = slice(j * 128, (j + 1) * 128)
            f, b, v, gate = of_heads(fs), of_heads(bs), of_heads(vs), of_heads(gs)
            recall = [seen[t, span, lanes] for t in range(T)]
            look = [seen[T + t, span, lanes] for t in range(T)]
            f01 = f[0] * f[1]
            f12 = f[1] * f[2]
            f012 = f01 * f[2]
            u0 = b[0] * (v[0] - f[0] * recall[0])
            u1 = b[1] * (v[1] - f01 * recall[1] - f[1] * k21 * u0)
            u2 = b[2] * (v[2] - f012 * recall[2] - f12 * k31 * u0 - f[2] * k32 * u1)
            c0 = f[0] * look[0] + qks[0][0] * u0
            c1 = f01 * look[1] + f[1] * qks[1][0] * u0 + qks[1][1] * u1
            c2 = f012 * look[2] + f12 * qks[2][0] * u0 + f[2] * qks[2][1] * u1 + qks[2][2] * u2
            late.append((f12 * u0, f[2] * u1, u2, f012))
            ready = []
            for t, c in enumerate((c0, c1, c2)):
                normed = c * lax.rsqrt(jnp.mean(c * c, axis=-1, keepdims=True) + EPSILON) * gain
                ready.append(normed * (gate[t] * (1.0 / (1.0 + jnp.exp(-gate[t])))))
            done.append(ready)

        for i in group:
            at = slice((i - first) * R, (i - first + 1) * R)
            outs.append(
                jnp.concatenate(
                    [jnp.concatenate([x[at] for x in done[j]], axis=0) for j in range(2)], axis=1
                ).astype(BF16)
            )
            ku_ref[i] = jnp.concatenate([x[i * R : (i + 1) * R] for x in kt], axis=0)
            for j in range(2):
                lanes = slice(j * 128, (j + 1) * 128)
                uu_ref[i, :, lanes] = jnp.concatenate([x[at] for x in late[j][:3]], axis=0)
                f3_ref[i, :, lanes] = late[j][3][at]
        for source, target in ((ku_ref, k_hbm_out), (uu_ref, u_hbm_out), (f3_ref, f_hbm_out)):
            span = pl.ds(first, count)
            written.append(
                pltpu.make_async_copy(
                    source.at[span], target.at[span], out_sem.at[len(written)]
                )
            )
            written[-1].start()
        arrive(2 * place + 1)
        for i in group:
            part = dot(outs[i], w_in[i * 256 : (i + 1) * 256, :])
            if i == 0:
                acc[...] = part
            elif i < HK - 1:
                acc[...] += part
            else:
                total = acc[...] + part
                send_ref[...] = total.astype(BF16)
                own_ref[...] = total + h_in[...].reshape(TOK, D).astype(F32)
    for copy in written:
        copy.wait()


def core_call(*args):
    args = [pltpu.with_memory_space_constraint(x, pltpu.HBM) for x in args]
    landing = [pltpu.VMEM(x.shape, x.dtype) for x in args[:10] + args[11:]]
    state = args[10]
    return pl.pallas_call(
        core_kernel,
        in_specs=[pl.BlockSpec(memory_space=pl.ANY)] * len(args),
        out_specs=[pl.BlockSpec(memory_space=pltpu.VMEM)] * 2
        + [pl.BlockSpec(memory_space=pl.ANY)] * 3,
        out_shape=[
            pltpu.VMEM((TOK, D), F32),
            pltpu.VMEM((TOK, D), BF16),
            pltpu.HBM((HK, TOK, 128), F32),
            pltpu.HBM((HK, TOK, 256), F32),
            pltpu.HBM((HK, R, 256), F32),
        ],
        scratch_shapes=landing
        + [pltpu.VMEM(state.shape, F32)]
        + [pltpu.VMEM((HK, rows, width), F32) for rows, width in ((TOK, 128), (TOK, 256), (R, 256))]
        + [pltpu.VMEM((HK * TOK, 128), F32)] * 2
        + [pltpu.VMEM((2 * HK * TOK, 128), F32)] * 4
        + [
            pltpu.VMEM((HK, 2 * TOK, R * 128), BF16),
            pltpu.VMEM((2 * T, HK * R, 256), F32),
            pltpu.VMEM((TOK, D), F32),
            pltpu.SemaphoreType.DMA((10,)),
            pltpu.SemaphoreType.DMA((2 * len(GROUPS),)),
            pltpu.SemaphoreType.DMA((3 * len(GROUPS),)),
        ],
        compiler_params=pltpu.CompilerParams(vmem_limit_bytes=CORE_VMEM * MiB),
        cost_estimate=pl.CostEstimate(flops=10**9, bytes_accessed=17 * MiB, transcendentals=10**5),
        name="core",
    )(*args)


def state_kernel(
    s_hbm, k_hbm, u_hbm, f_hbm, after_ref, o_hbm,
    state, k_in, u_in, f_in, small_sem, in_sem, out_sem,
):
    small = [
        pltpu.make_async_copy(source, target, small_sem.at[n])
        for n, (source, target) in enumerate(((k_hbm, k_in), (u_hbm, u_in), (f_hbm, f_in)))
    ]
    reads, writes = [], []
    for i in range(HK):
        heads = pl.ds(2 * i, 2)
        reads.append(pltpu.make_async_copy(s_hbm.at[:, heads], state.at[:, heads], in_sem.at[i]))
        writes.append(pltpu.make_async_copy(state.at[:, heads], o_hbm.at[:, heads], out_sem.at[i]))
    for copy in small + reads:
        copy.start()
    for copy in small:
        copy.wait()

    def split(x):
        high = x.astype(BF16).astype(F32)
        return high, x - high

    row_of = iota((128, 3 * TOK), 1) % R
    for i in range(HK):
        k_high, k_low = split(k_in[i])
        u_high, u_low = split(u_in[i])
        keys = jnp.concatenate([k_high, k_low, k_high], axis=0).T
        updates = jnp.concatenate([u_high, u_high, u_low], axis=0).astype(BF16)
        reads[i].wait()
        for r in range(R):
            own = jnp.where(row_of == r, keys, 0.0).astype(BF16)
            added = dot(own, updates)
            for j in range(2):
                lanes = slice(j * 128, (j + 1) * 128)
                state[r, 2 * i + j] = (
                    state[r, 2 * i + j] * f_in[i, r : r + 1, lanes] + added[:, lanes]
                )
        writes[i].start()
    for copy in writes:
        copy.wait()


def state_call(state, keys, updates, factor, after):
    args = [
        pltpu.with_memory_space_constraint(x, pltpu.HBM) for x in (state, keys, updates, factor)
    ]
    return pl.pallas_call(
        state_kernel,
        in_specs=[pl.BlockSpec(memory_space=pl.ANY)] * 5,
        out_specs=pl.BlockSpec(memory_space=pl.ANY),
        out_shape=pltpu.HBM(state.shape, F32),
        scratch_shapes=[pltpu.VMEM(x.shape, F32) for x in args]
        + [
            pltpu.SemaphoreType.DMA((3,)),
            pltpu.SemaphoreType.DMA((HK,)),
            pltpu.SemaphoreType.DMA((HK,)),
        ],
        compiler_params=pltpu.CompilerParams(vmem_limit_bytes=16 * MiB),
        cost_estimate=pl.CostEstimate(flops=10**9, bytes_accessed=17 * MiB, transcendentals=0),
        name="state",
    )(*args, pltpu.with_memory_space_constraint(after, pltpu.HBM))


def table_kernel(ids_ref, route_ref, state_ref, pick_ref, mix_ref):
    parity = lax.axis_index("hd")
    ids = ids_ref[...].reshape(TOK, -1)
    route = route_ref[...].reshape(TOK, -1)
    mixing = route / jnp.sum(route, axis=1, keepdims=True)
    expert = iota((TOK, CHIPS), 1) * 2 + parity
    named = jnp.zeros((TOK, CHIPS), F32)
    weight = jnp.zeros((TOK, CHIPS), F32)
    for c in range(ids.shape[1]):
        hit = ids[:, c : c + 1] == expert
        named = jnp.where(hit, 1.0, named)
        weight = jnp.where(hit, mixing[:, c : c + 1], weight)
    earlier = (iota((TOK, TOK), 0) > iota((TOK, TOK), 1)).astype(F32)
    rank = dot(earlier.astype(BF16), named.astype(BF16))
    rows = CHIPS * PARTS
    pad = jnp.zeros((TP - TOK, CHIPS), F32)
    spread = (iota((rows, CHIPS), 0) // PARTS == iota((rows, CHIPS), 1)).astype(F32).astype(BF16)
    across = (iota((CHIPS, rows), 1) // PARTS == iota((CHIPS, rows), 0)).astype(F32).astype(BF16)
    tile = (iota((TP, PARTS * TP), 1) % TP == iota((TP, PARTS * TP), 0)).astype(F32).astype(BF16)
    keep = iota((rows, PARTS * TP), 0) % PARTS == iota((rows, PARTS * TP), 1) // TP
    for s in range(SLOTS):
        here = jnp.where((named > 0.5) & (jnp.abs(rank - s) < 0.5), 1.0, 0.0)
        chosen = jnp.concatenate([here, pad], axis=0)
        tiled = dot(chosen.astype(BF16), tile, ((0,), (0,)))
        full = dot(spread, tiled.astype(BF16))
        pick_ref[s] = jnp.where(keep, full, 0.0).astype(BF16)
        share = jnp.concatenate([weight * here, pad], axis=0)
        high = share.astype(BF16).astype(F32)
        parts = jnp.concatenate([high, share - high], axis=0).astype(BF16)
        mix_ref[s] = dot(parts, across).astype(BF16)


def table_call(ids, route, state):
    return pl.pallas_call(
        table_kernel,
        in_specs=[pl.BlockSpec(memory_space=pltpu.VMEM)] * 2 + [pl.BlockSpec(memory_space=pl.ANY)],
        out_shape=[
            jax.ShapeDtypeStruct((SLOTS, CHIPS * PARTS, PARTS * TP), BF16),
            jax.ShapeDtypeStruct((SLOTS, 2 * TP, CHIPS * PARTS), BF16),
        ],
        compiler_params=pltpu.CompilerParams(vmem_limit_bytes=16 * MiB),
        cost_estimate=pl.CostEstimate(flops=10**8, bytes_accessed=10**6, transcendentals=0),
        name="tables",
    )(ids, route, pltpu.with_memory_space_constraint(state, pltpu.HBM))


def dispatch_kernel(own_ref, got_ref, gain_ref, pick_ref, res_ref, out_ref):
    residual = own_ref[...] + got_ref[...].astype(F32)
    res_ref[...] = residual
    scale = lax.rsqrt(jnp.mean(residual * residual, axis=1, keepdims=True) + EPSILON)
    normed = residual * scale * gain_ref[...]
    pad = jnp.zeros((TP - TOK, PC), F32)
    pieces = []
    for p in range(PARTS):
        pieces += [normed[:, p * PC : (p + 1) * PC], pad]
    stacked = jnp.concatenate(pieces, axis=0).astype(BF16)
    for s in range(SLOTS):
        out_ref[:, s * PC : (s + 1) * PC] = dot(pick_ref[s], stacked).astype(BF16)


def dispatch_call(own, got, gain, pick):
    return pl.pallas_call(
        dispatch_kernel,
        out_shape=[
            jax.ShapeDtypeStruct((TOK, D), F32),
            jax.ShapeDtypeStruct((CHIPS * PARTS, SLOTS * PC), BF16),
        ],
        compiler_params=pltpu.CompilerParams(vmem_limit_bytes=16 * MiB),
        cost_estimate=pl.CostEstimate(flops=2 * 10**8, bytes_accessed=2 * 10**6, transcendentals=0),
        name="dispatch",
    )(own, got, gain, pick)


def expert_kernel(x_ref, gate_ref, up_ref, down_ref, y_hbm, wide, y_out, sem):
    chunks = SLOTS * PC // 128
    for c in range(chunks):
        wide[c] = x_ref[:, c * 128 : (c + 1) * 128].astype(F32)
    gate = jnp.zeros((SLOTS * CHIPS, FF), F32)
    up = jnp.zeros((SLOTS * CHIPS, FF), F32)
    for p in range(PARTS):
        rows = [wide[c, pl.ds(p, CHIPS, stride=PARTS), :] for c in range(chunks)]
        x = jnp.concatenate(
            [jnp.concatenate(rows[0::2], axis=0), jnp.concatenate(rows[1::2], axis=0)], axis=1
        ).astype(BF16)
        gate += dot(x, gate_ref[0, p * PC : (p + 1) * PC, :])
        up += dot(x, up_ref[0, p * PC : (p + 1) * PC, :])
    activated = (gate * (1.0 / (1.0 + jnp.exp(-gate))) * up).astype(BF16)
    for p in range(PARTS):
        y = dot(activated, down_ref[0, :, p * PC : (p + 1) * PC])
        for c in range(chunks):
            at, side = c // 2 * CHIPS, c % 2 * 128
            wide[c, pl.ds(p, CHIPS, stride=PARTS), :] = y[at : at + CHIPS, side : side + 128]
    copies = []
    for c in range(chunks):
        lanes = slice(c * 128, (c + 1) * 128)
        y_out[:, lanes] = wide[c].astype(BF16)
        lanes = pl.ds(c * 128, 128)
        copies.append(pltpu.make_async_copy(y_out.at[:, lanes], y_hbm.at[:, lanes], sem.at[c]))
        copies[c].start()
    for copy in copies:
        copy.wait()


def expert_call(x, gate, up, down):
    return pl.pallas_call(
        expert_kernel,
        out_specs=pl.BlockSpec(memory_space=pl.ANY),
        out_shape=pltpu.HBM(x.shape, BF16),
        scratch_shapes=[
            pltpu.VMEM((x.shape[1] // 128, x.shape[0], 128), F32),
            pltpu.VMEM(x.shape, BF16),
            pltpu.SemaphoreType.DMA((x.shape[1] // 128,)),
        ],
        compiler_params=pltpu.CompilerParams(vmem_limit_bytes=24 * MiB),
        cost_estimate=pl.CostEstimate(
            flops=12 * 10**8, bytes_accessed=8 * 10**6, transcendentals=10**5
        ),
        name="expert",
    )(x, gate, up, down)


def combine_kernel(y_ref, mix_ref, res_ref, state_ref, keep_ref, send_ref, out_ref):
    parity = lax.axis_index("hd")
    part_of = iota((2 * TP, CHIPS * PARTS), 1) % PARTS
    half = D // 2
    total = None
    for s in range(SLOTS):
        mix = mix_ref[s].astype(F32)
        rows = [jnp.where(part_of == p, mix, 0.0) for p in range(PARTS)]
        lhs = jnp.concatenate(rows, axis=0).astype(BF16)
        one = dot(lhs, y_ref[:, s * PC : (s + 1) * PC])
        total = one if total is None else total + one
    parts = []
    for p in range(PARTS):
        at = p * 2 * TP
        parts.append(total[at : at + TOK] + total[at + TP : at + TP + TOK])
    low = jnp.concatenate(parts[: PARTS // 2], axis=1)
    high = jnp.concatenate(parts[PARTS // 2 :], axis=1)
    first = parity == 0
    keep_ref[...] = jnp.where(first, res_ref[:, :half] + low, res_ref[:, half:] + high)
    send_ref[...] = jnp.where(first, high, low).astype(BF16)


def combine_call(y, mix, residual, state):
    vmem = pl.BlockSpec(memory_space=pltpu.VMEM)
    held = pl.BlockSpec(memory_space=pl.ANY)
    return pl.pallas_call(
        combine_kernel,
        in_specs=[vmem, vmem, vmem, held],
        out_specs=[vmem, vmem, held],
        out_shape=[
            jax.ShapeDtypeStruct((TOK, D // 2), F32),
            jax.ShapeDtypeStruct((TOK, D // 2), BF16),
            pltpu.HBM(state.shape, F32),
        ],
        input_output_aliases={3: 2},
        compiler_params=pltpu.CompilerParams(vmem_limit_bytes=24 * MiB),
        cost_estimate=pl.CostEstimate(flops=4 * 10**8, bytes_accessed=10**6, transcendentals=0),
        name="combine",
    )(y, mix, residual, pltpu.with_memory_space_constraint(state, pltpu.HBM))


def local(
    hidden_in,
    new_queries,
    new_keys,
    new_values,
    out_gate,
    decay_logit,
    write_logit,
    decay_scale,
    decay_bias,
    head_gain,
    out_projection,
    norm_gain,
    expert_ids,
    route_weight,
    gate_weight,
    up_weight,
    down_weight,
    old_state,
):
    def by_step(x):
        return jnp.transpose(x, (1, 0, 2))

    own, send, keys, updates, factor = core_call(
        new_queries,
        new_keys,
        new_values,
        out_gate,
        by_step(decay_logit),
        by_step(write_logit),
        decay_scale.reshape(1, -1),
        decay_bias.reshape(1, -1),
        head_gain.reshape(1, -1),
        by_step(hidden_in),
        old_state,
        out_projection,
    )
    swap = [(0, 1), (1, 0)]
    got = lax.ppermute(send, "hd", swap)
    pick, mix = table_call(by_step(expert_ids), by_step(route_weight), old_state)
    residual, outbound = dispatch_call(own, got, norm_gain.reshape(1, -1), pick)
    shape = (CHIPS, PARTS, SLOTS * PC)
    arrived = lax.all_to_all(outbound.reshape(shape), "ep", 0, 0, tiled=True)
    produced = expert_call(arrived.reshape(outbound.shape), gate_weight, up_weight, down_weight)
    new_state = state_call(old_state, keys, updates, factor, produced)
    returned = lax.all_to_all(produced.reshape(shape), "ep", 0, 0, tiled=True)
    keep, give, new_state = combine_call(
        returned.reshape(outbound.shape), mix, residual, new_state
    )
    got = lax.ppermute(give, "hd", swap)
    total = keep + got.astype(F32)
    output_rows = by_step(total.astype(BF16).reshape(T, R, -1))
    return (output_rows, new_state)


def solution(mesh):
    in_specs = (
        P("ep", None, None),
        P("ep", None, "hd", None),
        P("ep", None, "hd", None),
        P("ep", None, "hd", None),
        P("ep", None, "hd", None),
        P("ep", None, "hd"),
        P("ep", None, "hd"),
        P("hd"),
        P("hd"),
        P(),
        P("hd", None),
        P(),
        P("ep", None, None),
        P("ep", None, None),
        P(("ep", "hd"), None, None),
        P(("ep", "hd"), None, None),
        P(("ep", "hd"), None, None),
        P("ep", "hd", None, None),
    )
    out_specs = (P("ep", None, "hd"), P("ep", "hd", None, None))
    return jax.shard_map(local, mesh=mesh, in_specs=in_specs, out_specs=out_specs, check_vma=False)
```

```python
import jax
import jax.numpy as jnp
from jax import lax
from jax.experimental import pallas as pl
from jax.experimental.pallas import tpu as pltpu
from jax.sharding import PartitionSpec as P

EPSILON = 1e-06
F32 = jnp.float32
BF16 = jnp.bfloat16

R = 8
T = 3
TOK = R * T
HK = 8
D = 2048
FF = 512
SLOTS = 3
CHIPS = 64
PARTS = 8
PC = D // PARTS
TP = 32
MiB = 1 << 20
CORE_VMEM = 62
GROUPS = (5, 3)
STARTS = tuple(sum(GROUPS[:n]) for n in range(len(GROUPS)))
OUT_PIECES = 8
AHEAD = 2


def dot(a, b, dims=((1,), (0,))):
    return lax.dot_general(a, b, (dims, ((), ())), preferred_element_type=F32)


def iota(shape, dim):
    return lax.broadcasted_iota(jnp.int32, shape, dim)


def core_kernel(
    q_hbm, k_hbm, v_hbm, g_hbm, a_hbm, b_hbm, scale_hbm, bias_hbm, gain_hbm, h_hbm, s_hbm, w_hbm,
    own_ref, send_ref, k_hbm_out, u_hbm_out, f_hbm_out,
    q_in, k_in, v_in, g_in, a_in, b_in, scale_in, bias_in, gain_in, h_in, w_in, state_ref, ku_ref, uu_ref, f3_ref,
    qs, ks, vs, gs, fs, bs, lhs, seen, acc, small_sem, stream_sem, out_sem,
):
    small = [
        pltpu.make_async_copy(source, target, small_sem.at[i])
        for i, (source, target) in enumerate(
            (
                (q_hbm, q_in),
                (k_hbm, k_in),
                (a_hbm, a_in),
                (b_hbm, b_in),
                (scale_hbm, scale_in),
                (bias_hbm, bias_in),
                (gain_hbm, gain_in),
                (v_hbm, v_in),
                (g_hbm, g_in),
                (h_hbm, h_in),
            )
        )
    ]
    stream = []
    for first, count in zip(STARTS, GROUPS):
        heads, rows = pl.ds(2 * first, 2 * count), pl.ds(256 * first, 256 * count)
        sems = (stream_sem.at[len(stream)], stream_sem.at[len(stream) + 1])
        stream += [
            pltpu.make_async_copy(s_hbm.at[:, heads], state_ref.at[:, heads], sems[0]),
            pltpu.make_async_copy(w_hbm.at[rows], w_in.at[rows], sems[1]),
        ]
    for copy in small + stream[:AHEAD]:
        copy.start()
    for copy in small:
        copy.wait()

    def arrive(n):
        stream[n].wait()
        if n + AHEAD < len(stream):
            stream[n + AHEAD].start()

    for t in range(T):
        for r in range(R):
            rows = pl.ds(t * HK * R + r, HK, stride=R)
            qs[rows, :] = q_in[r, t].astype(F32)
            ks[rows, :] = k_in[r, t].astype(F32)
            v = v_in[r, t].astype(F32)
            g = g_in[r, t].astype(F32)
            for half in range(2):
                rows = pl.ds((2 * t + half) * HK * R + r, HK, stride=R)
                vs[rows, :] = v[half * HK : (half + 1) * HK]
                gs[rows, :] = g[half * HK : (half + 1) * HK]
    rate = -jnp.exp(scale_in[...])
    for t in range(T):
        x = a_in[t].astype(F32) + bias_in[...]
        soft = jnp.maximum(x, 0.0) + jnp.log1p(jnp.exp(-jnp.abs(x)))
        factor = jnp.exp(rate * soft)
        strength = 1.0 / (1.0 + jnp.exp(-b_in[t].astype(F32)))
        for h in range(2 * HK):
            rows = slice((t * 2 * HK + h) * R, (t * 2 * HK + h + 1) * R)
            fs[rows, :] = jnp.broadcast_to(factor[:, h : h + 1], (R, 128))
            bs[rows, :] = jnp.broadcast_to(strength[:, h : h + 1], (R, 128))
    q = qs[...]
    k = ks[...]
    q = q * lax.rsqrt(jnp.sum(q * q, axis=-1, keepdims=True) + EPSILON)
    k = k * lax.rsqrt(jnp.sum(k * k, axis=-1, keepdims=True) + EPSILON)
    each = HK * R
    qt = [q[t * each : (t + 1) * each] for t in range(T)]
    kt = [k[t * each : (t + 1) * each] for t in range(T)]
    row_of = iota((2 * TOK, 128), 0) % R
    for i in range(HK):
        at = slice(i * R, (i + 1) * R)
        kq = jnp.concatenate([x[at] for x in kt + qt], axis=0)
        for r in range(R):
            lhs[i, :, r * 128 : (r + 1) * 128] = jnp.where(row_of == r, kq, 0.0).astype(BF16)

    def pair(x, y):
        return jnp.sum(x * y, axis=-1, keepdims=True)

    kk21, kk31, kk32 = pair(kt[1], kt[0]), pair(kt[2], kt[0]), pair(kt[2], kt[1])
    qk = [[pair(qt[t], kt[s]) for s in range(t + 1)] for t in range(T)]

    gain = gain_in[...]
    outs = []
    written = []
    for place, (first, count) in enumerate(zip(STARTS, GROUPS)):
        group = range(first, first + count)
        span = slice(first * R, (first + count) * R)
        arrive(2 * place)
        for i in group:
            state = jnp.concatenate(
                [state_ref[:, 2 * i + j].reshape(R * 128, 128).astype(BF16) for j in range(2)],
                axis=1,
            )
            both = dot(lhs[i], state)
            for part in range(2 * T):
                seen[part, i * R : (i + 1) * R, :] = both[part * R : (part + 1) * R]

        k21, k31, k32 = kk21[span], kk31[span], kk32[span]
        qks = [[x[span] for x in row] for row in qk]
        late = []
        done = []
        for j in range(2):

            def of_heads(ref):
                return [
                    jnp.concatenate(
                        [ref[pl.ds((t * 2 * HK + 2 * i + j) * R, R), :] for i in group], axis=0
                    )
                    for t in range(T)
                ]

            lanes = slice(j * 128, (j + 1) * 128)
            f, b, v, gate = of_heads(fs), of_heads(bs), of_heads(vs), of_heads(gs)
            recall = [seen[t, span, lanes] for t in range(T)]
            look = [seen[T + t, span, lanes] for t in range(T)]
            f01 = f[0] * f[1]
            f12 = f[1] * f[2]
            f012 = f01 * f[2]
            u0 = b[0] * (v[0] - f[0] * recall[0])
            u1 = b[1] * (v[1] - f01 * recall[1] - f[1] * k21 * u0)
            u2 = b[2] * (v[2] - f012 * recall[2] - f12 * k31 * u0 - f[2] * k32 * u1)
            c0 = f[0] * look[0] + qks[0][0] * u0
            c1 = f01 * look[1] + f[1] * qks[1][0] * u0 + qks[1][1] * u1
            c2 = f012 * look[2] + f12 * qks[2][0] * u0 + f[2] * qks[2][1] * u1 + qks[2][2] * u2
            late.append((f12 * u0, f[2] * u1, u2, f012))
            ready = []
            for t, c in enumerate((c0, c1, c2)):
                normed = c * lax.rsqrt(jnp.mean(c * c, axis=-1, keepdims=True) + EPSILON) * gain
                ready.append(normed * (gate[t] * (1.0 / (1.0 + jnp.exp(-gate[t])))))
            done.append(ready)

        for i in group:
            at = slice((i - first) * R, (i - first + 1) * R)
            outs.append(
                jnp.concatenate(
                    [jnp.concatenate([x[at] for x in done[j]], axis=0) for j in range(2)], axis=1
                ).astype(BF16)
            )
            ku_ref[i] = jnp.concatenate([x[i * R : (i + 1) * R] for x in kt], axis=0)
            for j in range(2):
                lanes = slice(j * 128, (j + 1) * 128)
                uu_ref[i, :, lanes] = jnp.concatenate([x[at] for x in late[j][:3]], axis=0)
                f3_ref[i, :, lanes] = late[j][3][at]
        for source, target in ((ku_ref, k_hbm_out), (uu_ref, u_hbm_out), (f3_ref, f_hbm_out)):
            span = pl.ds(first, count)
            written.append(
                pltpu.make_async_copy(
                    source.at[span], target.at[span], out_sem.at[len(written)]
                )
            )
            written[-1].start()
        arrive(2 * place + 1)
        for i in group:
            part = dot(outs[i], w_in[i * 256 : (i + 1) * 256, :])
            if i == 0:
                acc[...] = part
            elif i < HK - 1:
                acc[...] += part
            else:
                total = acc[...] + part
                send_ref[...] = total.astype(BF16)
                own_ref[...] = total + h_in[...].reshape(TOK, D).astype(F32)
    for copy in written:
        copy.wait()


def core_call(*args):
    args = [pltpu.with_memory_space_constraint(x, pltpu.HBM) for x in args]
    landing = [pltpu.VMEM(x.shape, x.dtype) for x in args[:10] + args[11:]]
    state = args[10]
    return pl.pallas_call(
        core_kernel,
        in_specs=[pl.BlockSpec(memory_space=pl.ANY)] * len(args),
        out_specs=[pl.BlockSpec(memory_space=pltpu.VMEM)] * 2
        + [pl.BlockSpec(memory_space=pl.ANY)] * 3,
        out_shape=[
            pltpu.VMEM((TOK, D), F32),
            pltpu.VMEM((TOK, D), BF16),
            pltpu.HBM((HK, TOK, 128), F32),
            pltpu.HBM((HK, TOK, 256), F32),
            pltpu.HBM((HK, R, 256), F32),
        ],
        scratch_shapes=landing
        + [pltpu.VMEM(state.shape, F32)]
        + [pltpu.VMEM((HK, rows, width), F32) for rows, width in ((TOK, 128), (TOK, 256), (R, 256))]
        + [pltpu.VMEM((HK * TOK, 128), F32)] * 2
        + [pltpu.VMEM((2 * HK * TOK, 128), F32)] * 4
        + [
            pltpu.VMEM((HK, 2 * TOK, R * 128), BF16),
            pltpu.VMEM((2 * T, HK * R, 256), F32),
            pltpu.VMEM((TOK, D), F32),
            pltpu.SemaphoreType.DMA((10,)),
            pltpu.SemaphoreType.DMA((2 * len(GROUPS),)),
            pltpu.SemaphoreType.DMA((3 * len(GROUPS),)),
        ],
        compiler_params=pltpu.CompilerParams(vmem_limit_bytes=CORE_VMEM * MiB),
        cost_estimate=pl.CostEstimate(flops=10**9, bytes_accessed=17 * MiB, transcendentals=10**5),
        name="core",
    )(*args)


def state_kernel(
    s_hbm, k_hbm, u_hbm, f_hbm, after_ref, o_hbm,
    state, k_in, u_in, f_in, small_sem, in_sem, out_sem,
):
    small = [
        pltpu.make_async_copy(source, target, small_sem.at[n])
        for n, (source, target) in enumerate(((k_hbm, k_in), (u_hbm, u_in), (f_hbm, f_in)))
    ]
    reads, writes = [], []
    for i in range(HK):
        heads = pl.ds(2 * i, 2)
        reads.append(pltpu.make_async_copy(s_hbm.at[:, heads], state.at[:, heads], in_sem.at[i]))
        writes.append(pltpu.make_async_copy(state.at[:, heads], o_hbm.at[:, heads], out_sem.at[i]))
    for copy in small + reads:
        copy.start()
    for copy in small:
        copy.wait()

    def split(x):
        high = x.astype(BF16).astype(F32)
        return high, x - high

    row_of = iota((128, 3 * TOK), 1) % R
    for i in range(HK):
        k_high, k_low = split(k_in[i])
        u_high, u_low = split(u_in[i])
        keys = jnp.concatenate([k_high, k_low, k_high], axis=0).T
        updates = jnp.concatenate([u_high, u_high, u_low], axis=0).astype(BF16)
        reads[i].wait()
        for r in range(R):
            own = jnp.where(row_of == r, keys, 0.0).astype(BF16)
            added = dot(own, updates)
            for j in range(2):
                lanes = slice(j * 128, (j + 1) * 128)
                state[r, 2 * i + j] = (
                    state[r, 2 * i + j] * f_in[i, r : r + 1, lanes] + added[:, lanes]
                )
        writes[i].start()
    for copy in writes:
        copy.wait()


def state_call(state, keys, updates, factor, after):
    args = [
        pltpu.with_memory_space_constraint(x, pltpu.HBM) for x in (state, keys, updates, factor)
    ]
    return pl.pallas_call(
        state_kernel,
        in_specs=[pl.BlockSpec(memory_space=pl.ANY)] * 5,
        out_specs=pl.BlockSpec(memory_space=pl.ANY),
        out_shape=pltpu.HBM(state.shape, F32),
        scratch_shapes=[pltpu.VMEM(x.shape, F32) for x in args]
        + [
            pltpu.SemaphoreType.DMA((3,)),
            pltpu.SemaphoreType.DMA((HK,)),
            pltpu.SemaphoreType.DMA((HK,)),
        ],
        compiler_params=pltpu.CompilerParams(vmem_limit_bytes=16 * MiB),
        cost_estimate=pl.CostEstimate(flops=10**9, bytes_accessed=17 * MiB, transcendentals=0),
        name="state",
    )(*args, pltpu.with_memory_space_constraint(after, pltpu.HBM))


def table_kernel(ids_ref, route_ref, state_ref, pick_ref, mix_ref):
    parity = lax.axis_index("hd")
    ids = ids_ref[...].reshape(TOK, -1)
    route = route_ref[...].reshape(TOK, -1)
    mixing = route / jnp.sum(route, axis=1, keepdims=True)
    expert = iota((TOK, CHIPS), 1) * 2 + parity
    named = jnp.zeros((TOK, CHIPS), F32)
    weight = jnp.zeros((TOK, CHIPS), F32)
    for c in range(ids.shape[1]):
        hit = ids[:, c : c + 1] == expert
        named = jnp.where(hit, 1.0, named)
        weight = jnp.where(hit, mixing[:, c : c + 1], weight)
    earlier = (iota((TOK, TOK), 0) > iota((TOK, TOK), 1)).astype(F32)
    rank = dot(earlier.astype(BF16), named.astype(BF16))
    rows = CHIPS * PARTS
    pad = jnp.zeros((TP - TOK, CHIPS), F32)
    spread = (iota((rows, CHIPS), 0) // PARTS == iota((rows, CHIPS), 1)).astype(F32).astype(BF16)
    across = (iota((CHIPS, rows), 1) // PARTS == iota((CHIPS, rows), 0)).astype(F32).astype(BF16)
    tile = (iota((TP, PARTS * TP), 1) % TP == iota((TP, PARTS * TP), 0)).astype(F32).astype(BF16)
    keep = iota((rows, PARTS * TP), 0) % PARTS == iota((rows, PARTS * TP), 1) // TP
    for s in range(SLOTS):
        here = jnp.where((named > 0.5) & (jnp.abs(rank - s) < 0.5), 1.0, 0.0)
        chosen = jnp.concatenate([here, pad], axis=0)
        tiled = dot(chosen.astype(BF16), tile, ((0,), (0,)))
        full = dot(spread, tiled.astype(BF16))
        pick_ref[s] = jnp.where(keep, full, 0.0).astype(BF16)
        share = jnp.concatenate([weight * here, pad], axis=0)
        high = share.astype(BF16).astype(F32)
        parts = jnp.concatenate([high, share - high], axis=0).astype(BF16)
        mix_ref[s] = dot(parts, across).astype(BF16)


def table_call(ids, route, state):
    return pl.pallas_call(
        table_kernel,
        in_specs=[pl.BlockSpec(memory_space=pltpu.VMEM)] * 2 + [pl.BlockSpec(memory_space=pl.ANY)],
        out_shape=[
            jax.ShapeDtypeStruct((SLOTS, CHIPS * PARTS, PARTS * TP), BF16),
            jax.ShapeDtypeStruct((SLOTS, 2 * TP, CHIPS * PARTS), BF16),
        ],
        compiler_params=pltpu.CompilerParams(vmem_limit_bytes=16 * MiB),
        cost_estimate=pl.CostEstimate(flops=10**8, bytes_accessed=10**6, transcendentals=0),
        name="tables",
    )(ids, route, pltpu.with_memory_space_constraint(state, pltpu.HBM))


def dispatch_kernel(own_ref, got_ref, gain_ref, pick_ref, res_ref, out_ref):
    residual = own_ref[...] + got_ref[...].astype(F32)
    res_ref[...] = residual
    scale = lax.rsqrt(jnp.mean(residual * residual, axis=1, keepdims=True) + EPSILON)
    normed = residual * scale * gain_ref[...]
    pad = jnp.zeros((TP - TOK, PC), F32)
    pieces = []
    for p in range(PARTS):
        pieces += [normed[:, p * PC : (p + 1) * PC], pad]
    stacked = jnp.concatenate(pieces, axis=0).astype(BF16)
    for s in range(SLOTS):
        out_ref[:, s * PC : (s + 1) * PC] = dot(pick_ref[s], stacked).astype(BF16)


def dispatch_call(own, got, gain, pick):
    return pl.pallas_call(
        dispatch_kernel,
        out_shape=[
            jax.ShapeDtypeStruct((TOK, D), F32),
            jax.ShapeDtypeStruct((CHIPS * PARTS, SLOTS * PC), BF16),
        ],
        compiler_params=pltpu.CompilerParams(vmem_limit_bytes=16 * MiB),
        cost_estimate=pl.CostEstimate(flops=2 * 10**8, bytes_accessed=2 * 10**6, transcendentals=0),
        name="dispatch",
    )(own, got, gain, pick)


def expert_kernel(x_ref, gate_ref, up_ref, down_ref, y_hbm, wide, y_out, sem):
    chunks = SLOTS * PC // 128
    for c in range(chunks):
        wide[c] = x_ref[:, c * 128 : (c + 1) * 128].astype(F32)
    gate = jnp.zeros((SLOTS * CHIPS, FF), F32)
    up = jnp.zeros((SLOTS * CHIPS, FF), F32)
    for p in range(PARTS):
        rows = [wide[c, pl.ds(p, CHIPS, stride=PARTS), :] for c in range(chunks)]
        x = jnp.concatenate(
            [jnp.concatenate(rows[0::2], axis=0), jnp.concatenate(rows[1::2], axis=0)], axis=1
        ).astype(BF16)
        gate += dot(x, gate_ref[0, p * PC : (p + 1) * PC, :])
        up += dot(x, up_ref[0, p * PC : (p + 1) * PC, :])
    activated = (gate * (1.0 / (1.0 + jnp.exp(-gate))) * up).astype(BF16)
    for p in range(PARTS):
        y = dot(activated, down_ref[0, :, p * PC : (p + 1) * PC])
        for c in range(chunks):
            at, side = c // 2 * CHIPS, c % 2 * 128
            wide[c, pl.ds(p, CHIPS, stride=PARTS), :] = y[at : at + CHIPS, side : side + 128]
    copies = []
    rows_out = x_ref.shape[0] // OUT_PIECES
    for n in range(OUT_PIECES):
        rows = slice(n * rows_out, (n + 1) * rows_out)
        for c in range(chunks):
            y_out[rows, c * 128 : (c + 1) * 128] = wide[c, rows].astype(BF16)
        rows = pl.ds(n * rows_out, rows_out)
        copies.append(pltpu.make_async_copy(y_out.at[rows], y_hbm.at[rows], sem.at[n]))
        copies[n].start()
    for copy in copies:
        copy.wait()


def expert_call(x, gate, up, down):
    return pl.pallas_call(
        expert_kernel,
        out_specs=pl.BlockSpec(memory_space=pl.ANY),
        out_shape=pltpu.HBM(x.shape, BF16),
        scratch_shapes=[
            pltpu.VMEM((x.shape[1] // 128, x.shape[0], 128), F32),
            pltpu.VMEM(x.shape, BF16),
            pltpu.SemaphoreType.DMA((OUT_PIECES,)),
        ],
        compiler_params=pltpu.CompilerParams(vmem_limit_bytes=24 * MiB),
        cost_estimate=pl.CostEstimate(
            flops=12 * 10**8, bytes_accessed=8 * 10**6, transcendentals=10**5
        ),
        name="expert",
    )(x, gate, up, down)


def combine_kernel(y_ref, mix_ref, res_ref, state_ref, keep_ref, send_ref, out_ref):
    parity = lax.axis_index("hd")
    part_of = iota((2 * TP, CHIPS * PARTS), 1) % PARTS
    half = D // 2
    total = None
    for s in range(SLOTS):
        mix = mix_ref[s].astype(F32)
        rows = [jnp.where(part_of == p, mix, 0.0) for p in range(PARTS)]
        lhs = jnp.concatenate(rows, axis=0).astype(BF16)
        one = dot(lhs, y_ref[:, s * PC : (s + 1) * PC])
        total = one if total is None else total + one
    parts = []
    for p in range(PARTS):
        at = p * 2 * TP
        parts.append(total[at : at + TOK] + total[at + TP : at + TP + TOK])
    low = jnp.concatenate(parts[: PARTS // 2], axis=1)
    high = jnp.concatenate(parts[PARTS // 2 :], axis=1)
    first = parity == 0
    keep_ref[...] = jnp.where(first, res_ref[:, :half] + low, res_ref[:, half:] + high)
    send_ref[...] = jnp.where(first, high, low).astype(BF16)


def combine_call(y, mix, residual, state):
    vmem = pl.BlockSpec(memory_space=pltpu.VMEM)
    held = pl.BlockSpec(memory_space=pl.ANY)
    return pl.pallas_call(
        combine_kernel,
        in_specs=[vmem, vmem, vmem, held],
        out_specs=[vmem, vmem, held],
        out_shape=[
            jax.ShapeDtypeStruct((TOK, D // 2), F32),
            jax.ShapeDtypeStruct((TOK, D // 2), BF16),
            pltpu.HBM(state.shape, F32),
        ],
        input_output_aliases={3: 2},
        compiler_params=pltpu.CompilerParams(vmem_limit_bytes=24 * MiB),
        cost_estimate=pl.CostEstimate(flops=4 * 10**8, bytes_accessed=10**6, transcendentals=0),
        name="combine",
    )(y, mix, residual, pltpu.with_memory_space_constraint(state, pltpu.HBM))


def local(
    hidden_in,
    new_queries,
    new_keys,
    new_values,
    out_gate,
    decay_logit,
    write_logit,
    decay_scale,
    decay_bias,
    head_gain,
    out_projection,
    norm_gain,
    expert_ids,
    route_weight,
    gate_weight,
    up_weight,
    down_weight,
    old_state,
):
    def by_step(x):
        return jnp.transpose(x, (1, 0, 2))

    own, send, keys, updates, factor = core_call(
        new_queries,
        new_keys,
        new_values,
        out_gate,
        by_step(decay_logit),
        by_step(write_logit),
        decay_scale.reshape(1, -1),
        decay_bias.reshape(1, -1),
        head_gain.reshape(1, -1),
        by_step(hidden_in),
        old_state,
        out_projection,
    )
    swap = [(0, 1), (1, 0)]
    got = lax.ppermute(send, "hd", swap)
    pick, mix = table_call(by_step(expert_ids), by_step(route_weight), old_state)
    residual, outbound = dispatch_call(own, got, norm_gain.reshape(1, -1), pick)
    shape = (CHIPS, PARTS, SLOTS * PC)
    arrived = lax.all_to_all(outbound.reshape(shape), "ep", 0, 0, tiled=True)
    produced = expert_call(arrived.reshape(outbound.shape), gate_weight, up_weight, down_weight)
    new_state = state_call(old_state, keys, updates, factor, produced)
    returned = lax.all_to_all(produced.reshape(shape), "ep", 0, 0, tiled=True)
    keep, give, new_state = combine_call(
        returned.reshape(outbound.shape), mix, residual, new_state
    )
    got = lax.ppermute(give, "hd", swap)
    total = keep + got.astype(F32)
    output_rows = by_step(total.astype(BF16).reshape(T, R, -1))
    return (output_rows, new_state)


def solution(mesh):
    in_specs = (
        P("ep", None, None),
        P("ep", None, "hd", None),
        P("ep", None, "hd", None),
        P("ep", None, "hd", None),
        P("ep", None, "hd", None),
        P("ep", None, "hd"),
        P("ep", None, "hd"),
        P("hd"),
        P("hd"),
        P(),
        P("hd", None),
        P(),
        P("ep", None, None),
        P("ep", None, None),
        P(("ep", "hd"), None, None),
        P(("ep", "hd"), None, None),
        P(("ep", "hd"), None, None),
        P("ep", "hd", None, None),
    )
    out_specs = (P("ep", None, "hd"), P("ep", "hd", None, None))
    return jax.shard_map(local, mesh=mesh, in_specs=in_specs, out_specs=out_specs, check_vma=False)
```
